256 devices in a mesh: rep: 2 (over core), own: 128 (over z, x, y).
Axes of the slice: x: 4, y: 4, z: 8, core: 2. Of those that a mesh axis runs over, the one named last changes fastest.
Arguments:
- embeddings: bfloat16 [65536, 1024], P(('rep', 'own'))
- cluster: int32 [65536], P(('rep', 'own')), may hold values from 0 to 511, as said below
- order: int32 [65536], P(('rep', 'own')), may hold values from 0 to 65535, each once
Outputs:
- nearest: float32 [65536], P(('rep', 'own'))
The draws below stay inside these ranges and needn't reach their ends.
Inputs may be any that keep to these rules, and one draw needn't show every extreme that they name: `cluster`: cluster c belongs to owner c // 4. In each aligned block of 256 rows (the rows of one device) at most 4 rows name clusters of one owner; in every block exactly 4 rows name clusters of one owner that is the same for all blocks. `order`: Distinct.
All inputs are finite; a program needn't handle non-finite values.
Results may differ from the reference program's by a relative error of at most 0.0005.
Values may be sent and summed in bfloat16 or wider, within the bound.
A program may use at most 64 MiB of HBM per device.

```python
import jax
import jax.numpy as jnp
from jax import lax

D = 1024
ROW_DEV = 256
CL_DEV = 4
CAP = 4
CLUSTERS = 512
ROWS = 65536
N_REP = 2
N_OWN = 128


def cluster_rows(key):
    random_key_list = jax.random.split(jax.random.fold_in(key, 11), 6)
    blocks = N_REP * N_OWN
    position_table = N_OWN * CAP
    loaded_owner_index = jax.random.randint(random_key_list[0], (), 0, N_OWN)
    extra_score_boost = jax.random.randint(random_key_list[1], (N_OWN,), 0, 4096)
    extra_score_boost = jnp.where(jnp.arange(N_OWN) == loaded_owner_index, 8192, extra_score_boost)
    position_owner = jnp.arange(position_table) // CAP
    random_fraction = jax.random.randint(random_key_list[2], (blocks, position_table), 0, 4096)
    score_values = (random_fraction + extra_score_boost[position_owner][None, :]) * position_table + jnp.arange(position_table)[None, :]
    unused, picked = lax.top_k(score_values, ROW_DEV)
    owners = picked // CAP
    shuffles = jax.vmap(lambda small_key: jax.random.permutation(small_key, ROW_DEV))(jax.random.split(random_key_list[3], blocks))
    owners = jnp.take_along_axis(owners, shuffles, axis=1)
    within = jnp.minimum(jax.random.randint(random_key_list[4], (blocks, ROW_DEV), 0, CL_DEV), jax.random.randint(random_key_list[5], (blocks, ROW_DEV), 0, CL_DEV))
    return (owners * CL_DEV + within).reshape(-1).astype(jnp.int32)


def draw_cluster(key, part):
    shared = cluster_rows(key)
    return shared


def draw_embeddings(key, part):
    shared = cluster_rows(key)
    key = jax.random.fold_in(key, 7)
    random_key_list = jax.random.split(key, 3)
    centres = jax.random.normal(random_key_list[0], (CLUSTERS, D), jnp.float32)
    tightness = jnp.exp(jax.random.uniform(random_key_list[1], (CLUSTERS,), jnp.float32, jnp.log(0.3), jnp.log(1.5)))
    centred = tightness[shared][:, None] * centres[shared]
    noise = jax.random.normal(random_key_list[2], (ROWS, D), jnp.float32)
    values = centred + noise
    return values.astype(jnp.bfloat16)


def setup_inputs(seed: int = 0) -> dict:
    key_of = jax.random.split(jax.random.key(seed), 4)
    embeddings = draw_embeddings(jax.random.fold_in(key_of[3], 71), 0)
    cluster = draw_cluster(jax.random.fold_in(key_of[3], 71), 0)
    order = jax.random.permutation(key_of[2], ROWS).astype(jnp.int32)
    return dict(embeddings=embeddings, cluster=cluster, order=order)


def reference(embeddings, cluster, order):
    values = embeddings.astype(jnp.float32)
    scale = lax.rsqrt(lax.optimization_barrier(jnp.sum(values * values, axis=-1, keepdims=True)) + 1e-06)
    unit_rows = (values * scale).astype(jnp.bfloat16)
    sort_key = cluster * ROWS + order
    ranking = jnp.argsort(sort_key).astype(jnp.int32)
    sorted_unit = unit_rows[ranking]
    sorted_cluster = cluster[ranking]
    sorted_order = order[ranking]
    span_rows = N_REP * N_OWN * CAP
    block_rows = min(512, ROWS)
    padded_unit = jnp.concatenate([jnp.zeros((span_rows, D), sorted_unit.dtype), sorted_unit], axis=0)
    padded_cluster = jnp.concatenate([jnp.full((span_rows,), -1, jnp.int32), sorted_cluster.astype(jnp.int32)], axis=0)
    padded_order = jnp.concatenate([jnp.zeros((span_rows,), jnp.int32), sorted_order.astype(jnp.int32)], axis=0)

    def one_block(block_index):
        first = (block_index * block_rows).astype(jnp.int32)
        query_unit = lax.dynamic_slice_in_dim(sorted_unit, first, block_rows, 0)
        query_cluster = lax.dynamic_slice_in_dim(sorted_cluster, first, block_rows, 0)
        query_order = lax.dynamic_slice_in_dim(sorted_order, first, block_rows, 0)
        key_unit = lax.dynamic_slice_in_dim(padded_unit, first, span_rows + block_rows, 0)
        key_cluster = lax.dynamic_slice_in_dim(padded_cluster, first, span_rows + block_rows, 0)
        key_order = lax.dynamic_slice_in_dim(padded_order, first, span_rows + block_rows, 0)
        similar = jnp.dot(query_unit, key_unit.T, preferred_element_type=jnp.float32)
        allowed = (key_cluster[None, :] == query_cluster[:, None]) & (key_order[None, :] < query_order[:, None])
        return lax.optimization_barrier(jnp.max(jnp.where(allowed, similar, -1.0), axis=1))
    sorted_best = lax.map(one_block, jnp.arange(ROWS // block_rows, dtype=jnp.int32)).reshape(-1)
    nearest = jnp.zeros((ROWS,), sorted_best.dtype).at[ranking].set(sorted_best)
    return nearest
```

```python
import jax
import jax.numpy as jnp
from jax import lax
from jax.experimental import pallas as pl
from jax.experimental.pallas import tpu as pltpu
from jax.sharding import PartitionSpec as P

MESH = pl.DeviceIdType.MESH
CL_DEV = 4
CAP = 4
NZ, NX, NY = 8, 4, 4
OWN = NZ * NX * NY
PLANE = NX * NY
ROWS = 256
D = 1024
SLOTS = OWN * CAP
WIDE = D // 4
MSG = 16
GROUP = PLANE * MSG
Z_ORDER = (4, 3, 5, 2, 6, 1, 7, 0)


def peer_of(me, dz, dx, dy):
    z, x, y = me // PLANE, (me // NY) % NX, me % NY
    return ((z + dz) % NZ) * PLANE + ((x + dx) % NX) * NY + (y + dy) % NY


def iota(shape, dim):
    return lax.broadcasted_iota(jnp.int32, shape, dim)


def column_of(row, eye):
    return jnp.sum(jnp.where(eye, row, 0), axis=1, keepdims=True)


def exact_dot(a, b):
    return jnp.dot(a, b, precision=lax.Precision.HIGHEST, preferred_element_type=jnp.float32)


def unpack_group(src, dst, src_row, dst_row):
    block = src[pl.ds(src_row, GROUP), :].astype(jnp.float32).reshape(PLANE // 2, 2, 2, 8, WIDE)
    low = iota((1, 8, WIDE), 1) < CAP
    for half in range(2):
        even, odd = block[:, 0, half], block[:, 1, half]
        first = jnp.where(low, even, jnp.roll(odd, CAP, axis=1))
        second = jnp.where(low, jnp.roll(even, CAP, axis=1), odd)
        for i, part in enumerate((first, second)):
            lane = (2 * half + i) * WIDE
            dst[pl.ds(dst_row, PLANE * CAP), lane : lane + WIDE] = part.reshape(PLANE * CAP, WIDE).astype(jnp.bfloat16)


def slot_codes(meta, base):
    table = meta[...].reshape(OWN, 128).astype(jnp.float32)
    spread = (iota((SLOTS, OWN), 0) // CAP == iota((SLOTS, OWN), 1)).astype(jnp.float32)
    wide = exact_dot(spread, table)
    pick = iota((SLOTS, 128), 1) == base + iota((SLOTS, 128), 0) % CAP
    column = jnp.sum(jnp.where(pick, wide, 0.0), axis=1, keepdims=True)
    spread_t = (iota((OWN, SLOTS), 1) // CAP == iota((OWN, SLOTS), 0)).astype(jnp.float32)
    tall = exact_dot(table.T, spread_t)
    pick_t = iota((128, SLOTS), 0) == base + iota((128, SLOTS), 1) % CAP
    row = jnp.sum(jnp.where(pick_t, tall, 0.0), axis=0, keepdims=True)
    return column, row


def kernel(
    emb, cl_ref, ord_ref, out_ref,
    x_vm, send, recv, recv2, unit_q, unit_k, meta_s, meta_r, meta_r2, res_s, res_r, key_code,
    in_sem, pay_s, pay_r, meta_ss, meta_rs, res_ss, res_rs, fwd_s, fwd_r, mfwd_s, mfwd_r,
):
    rep, me = lax.axis_index("rep"), lax.axis_index("own")
    my_z = me // PLANE
    other = 1 - rep
    base = (me % 32) * CAP

    load = pltpu.make_async_copy(emb, x_vm, in_sem)
    load.start()
    barrier = pltpu.get_barrier_semaphore()
    pl.semaphore_signal(barrier, inc=1, device_id=(other, me), device_id_type=MESH)

    def greet(k, carry):
        to = peer_of(me, k // PLANE, (k // NY) % NX, k % NY)
        pl.semaphore_signal(barrier, inc=1, device_id=(rep, to), device_id_type=MESH)
        return carry

    lax.fori_loop(1, OWN, greet, 0)

    cl_row, ord_row = cl_ref[...], ord_ref[...]
    square = (ROWS, ROWS)
    eye = iota(square, 0) == iota(square, 1)
    own_row = cl_row // CL_DEV
    own_col = column_of(own_row, eye)
    earlier = (own_col == own_row) & (iota(square, 0) < iota(square, 1))
    slot_row = jnp.sum(earlier.astype(jnp.int32), axis=0, keepdims=True)
    placed_row = own_row * CAP + slot_row
    code_row = (cl_row % CL_DEV) * 65536 + ord_row
    placed_col = column_of(placed_row, eye)
    code_col = column_of(code_row, eye)
    sent = placed_col == iota((ROWS, SLOTS), 1)
    codes = jnp.sum(jnp.where(sent, code_col + 1, 0), axis=0, keepdims=True) - 1
    for c in range(4):
        meta_s[c] = codes[:, 128 * c : 128 * c + 128]

    load.wait()
    values = x_vm[...].astype(jnp.float32)
    scale = lax.rsqrt(jnp.sum(values * values, axis=1, keepdims=True) + 1e-06)
    unit = (values * scale).astype(jnp.bfloat16)
    place = (iota((SLOTS, ROWS), 0) == placed_row).astype(jnp.bfloat16)
    low = iota((1, 8, WIDE), 1) < CAP
    evens, odds = [], []
    for half in range(2):
        first, second = (
            jnp.dot(place, unit[:, q * WIDE : (q + 1) * WIDE], preferred_element_type=jnp.float32).reshape(
                OWN // 2, 8, WIDE
            )
            for q in (2 * half, 2 * half + 1)
        )
        evens.append(jnp.where(low, first, jnp.roll(second, CAP, axis=1)))
        odds.append(jnp.where(low, jnp.roll(first, CAP, axis=1), second))
    packed = jnp.stack([jnp.stack(evens, axis=1), jnp.stack(odds, axis=1)], axis=1)
    send[...] = packed.reshape(OWN * MSG, WIDE).astype(jnp.bfloat16)

    pl.semaphore_wait(barrier, OWN)

    def send_meta(k, carry):
        to = peer_of(me, k // PLANE, (k // NY) % NX, k % NY)
        pltpu.make_async_remote_copy(
            src_ref=meta_s.at[to // 32], dst_ref=meta_r.at[me], send_sem=meta_ss, recv_sem=meta_rs,
            device_id=(rep, to), device_id_type=MESH,
        ).start()
        return carry

    lax.fori_loop(1, OWN, send_meta, 0)
    for dz in Z_ORDER:

        def send_block(k, carry, dz=dz):
            to = peer_of(me, dz, k // NY, k % NY)
            pltpu.make_async_remote_copy(
                src_ref=send.at[pl.ds(pl.multiple_of(to * MSG, MSG), MSG)],
                dst_ref=recv.at[pl.ds(pl.multiple_of(me * MSG, MSG), MSG)],
                send_sem=pay_s, recv_sem=pay_r.at[dz], device_id=(rep, to), device_id_type=MESH,
            ).start()
            return carry

        lax.fori_loop(1 if dz == 0 else 0, PLANE, send_block, 0)

    mine = pl.ds(pl.multiple_of(me * MSG, MSG), MSG)
    recv[mine, :] = send[mine, :]
    meta_r[me] = meta_s[me // 32]

    def landed(ref, n, sem):
        part = ref.at[pl.ds(0, n)]
        pltpu.make_async_copy(part, part, sem).wait()

    landed(meta_r, OWN - 1, meta_rs)
    landed(meta_r, OWN - 1, meta_ss)
    meta_fwd = pltpu.make_async_remote_copy(
        src_ref=meta_r, dst_ref=meta_r2, send_sem=mfwd_s, recv_sem=mfwd_r,
        device_id=(other, me), device_id_type=MESH,
    )
    meta_fwd.start()
    key_code[pl.ds(0, SLOTS), :], query_row = (lambda c, r: (jnp.broadcast_to(c, (SLOTS, 128)), r))(
        *slot_codes(meta_r, base)
    )
    meta_fwd.wait()
    key_code[pl.ds(SLOTS, SLOTS), :] = jnp.broadcast_to(slot_codes(meta_r2, base)[0], (SLOTS, 128))
    query_low = jnp.floor(query_row * (1.0 / 65536)) * 65536

    forwards = []
    for dz in Z_ORDER:
        z = (my_z + NZ - dz) % NZ
        start = pl.multiple_of(z * GROUP, GROUP)
        landed(recv, GROUP - (MSG if dz == 0 else 0), pay_r.at[dz])
        forward = pltpu.make_async_remote_copy(
            src_ref=recv.at[pl.ds(start, GROUP)], dst_ref=recv2.at[pl.ds(start, GROUP)],
            send_sem=fwd_s.at[dz], recv_sem=fwd_r.at[dz], device_id=(other, me), device_id_type=MESH,
        )
        forward.start()
        forwards.append((forward, z, start))
        unpack_group(recv, unit_q, start, pl.multiple_of(z * PLANE * CAP, PLANE * CAP))
    for forward, z, start in forwards:
        forward.wait()
        unpack_group(recv2, unit_k, start, pl.multiple_of(z * PLANE * CAP, PLANE * CAP))

    best = jnp.full((8, SLOTS), -1.0, jnp.float32)
    for side, keys in enumerate((unit_q, unit_k)):
        for b in range(2):
            similar = lax.dot_general(
                keys[pl.ds(256 * b, 256), :], unit_q[...], (((1,), (1,)), ((), ())),
                preferred_element_type=jnp.float32,
            )
            code = key_code[pl.ds(SLOTS * side + 256 * b, 256), 0:1]
            allowed = (code >= query_low) & (code < query_row)
            similar = jnp.where(allowed, similar, -1.0).reshape(32, 8, SLOTS)
            best = jnp.maximum(best, jnp.max(similar, axis=0))
    best = jnp.max(best, axis=0, keepdims=True)
    for c in range(4):
        res_s[c] = best[:, 128 * c : 128 * c + 128]

    def send_best(k, carry):
        to = peer_of(me, k // PLANE, (k // NY) % NX, k % NY)
        pltpu.make_async_remote_copy(
            src_ref=res_s.at[to // 32], dst_ref=res_r.at[me], send_sem=res_ss, recv_sem=res_rs,
            device_id=(rep, to), device_id_type=MESH,
        ).start()
        return carry

    lax.fori_loop(1, OWN, send_best, 0)
    res_r[me] = res_s[me // 32]
    landed(send, (OWN - 1) * MSG, pay_s)
    landed(res_r, OWN - 1, res_ss)
    landed(res_r, OWN - 1, res_rs)

    home = res_r[...].reshape(OWN, 128)
    lane = iota((OWN, 128), 1)
    owner_here = iota((OWN, ROWS), 0) == own_row
    nearest = jnp.zeros((OWN, ROWS), jnp.float32)
    for s in range(CAP):
        value = jnp.sum(jnp.where(lane == base + s, home, 0.0), axis=1, keepdims=True)
        nearest = jnp.where(owner_here & (slot_row == s), value, nearest)
    out_ref[...] = jnp.sum(nearest, axis=0, keepdims=True)


def body(embeddings, cluster, order):
    vmem = pl.BlockSpec(memory_space=pltpu.VMEM)
    dma = pltpu.SemaphoreType.DMA
    result = pl.pallas_call(
        kernel,
        out_shape=jax.ShapeDtypeStruct((1, ROWS), jnp.float32),
        in_specs=[pl.BlockSpec(memory_space=pl.ANY), vmem, vmem],
        out_specs=vmem,
        scratch_shapes=[
            pltpu.VMEM((ROWS, D), jnp.bfloat16),
            pltpu.VMEM((OWN * MSG, WIDE), jnp.bfloat16),
            pltpu.VMEM((OWN * MSG, WIDE), jnp.bfloat16),
            pltpu.VMEM((OWN * MSG, WIDE), jnp.bfloat16),
            pltpu.VMEM((SLOTS, D), jnp.bfloat16),
            pltpu.VMEM((SLOTS, D), jnp.bfloat16),
            pltpu.VMEM((4, 1, 128), jnp.int32),
            pltpu.VMEM((OWN, 1, 128), jnp.int32),
            pltpu.VMEM((OWN, 1, 128), jnp.int32),
            pltpu.VMEM((4, 1, 128), jnp.float32),
            pltpu.VMEM((OWN, 1, 128), jnp.float32),
            pltpu.VMEM((2 * SLOTS, 128), jnp.float32),
            dma, dma, dma((NZ,)), dma, dma, dma, dma, dma((NZ,)), dma((NZ,)), dma, dma,
        ],
        compiler_params=pltpu.CompilerParams(
            collective_id=0, has_side_effects=True, vmem_limit_bytes=48 * 2**20
        ),
    )(embeddings, cluster.reshape(1, ROWS), order.reshape(1, ROWS))
    return result.reshape(ROWS)


def solution(mesh):
    placed = (P(("rep", "own"), None), P(("rep", "own")), P(("rep", "own")))
    return jax.shard_map(body, mesh=mesh, in_specs=placed, out_specs=P(("rep", "own")), check_vma=False)
```

```python
import jax
import jax.numpy as jnp
from jax import lax
from jax.experimental import pallas as pl
from jax.experimental.pallas import tpu as pltpu
from jax.sharding import PartitionSpec as P

MESH = pl.DeviceIdType.MESH
CL_DEV = 4
CAP = 4
NZ, NX, NY = 8, 4, 4
OWN = NZ * NX * NY
PLANE = NX * NY
ROWS = 256
D = 1024
SLOTS = OWN * CAP
WIDE = D // 4
MSG = 16
GROUP = PLANE * MSG
TILE = PLANE * CAP
Z_ORDER = (4, 3, 5, 2, 6, 1, 7, 0)
PLANE_ORDER = ((2, 2), (2, 1), (1, 2), (2, 3), (3, 2), (1, 1), (3, 3), (1, 3), (3, 1), (2, 0), (0, 2), (1, 0), (0, 1), (3, 0), (0, 3), (0, 0))


def iota(shape, dim):
    return lax.broadcasted_iota(jnp.int32, shape, dim)


def column_of(row, eye):
    return jnp.sum(jnp.where(eye, row, 0), axis=1, keepdims=True)


def exact_dot(a, b):
    return jnp.dot(a, b, precision=lax.Precision.HIGHEST, preferred_element_type=jnp.float32)


def unpack_group(src, dst, src_row, dst_row):
    block = src[pl.ds(src_row, GROUP), :].astype(jnp.float32).reshape(PLANE // 2, 2, 2, 8, WIDE)
    low = iota((1, 8, WIDE), 1) < CAP
    for half in range(2):
        even, odd = block[:, 0, half], block[:, 1, half]
        first = jnp.where(low, even, jnp.roll(odd, CAP, axis=1))
        second = jnp.where(low, jnp.roll(even, CAP, axis=1), odd)
        for i, part in enumerate((first, second)):
            lane = (2 * half + i) * WIDE
            dst[pl.ds(dst_row, TILE), lane : lane + WIDE] = part.reshape(TILE, WIDE).astype(jnp.bfloat16)


def source_row(slot):
    source = slot // CAP
    return (source % NY * NX + source // NY % NX) * NZ + source // PLANE


def slot_column(table, base):
    spread = (source_row(iota((SLOTS, OWN), 0)) == iota((SLOTS, OWN), 1)).astype(jnp.float32)
    pick = iota((SLOTS, 128), 1) == base + iota((SLOTS, 128), 0) % CAP
    column = jnp.sum(jnp.where(pick, exact_dot(spread, table), 0.0), axis=1, keepdims=True)
    return jnp.broadcast_to(column, (SLOTS, 128))


def slot_row_of(table, base):
    spread = (source_row(iota((OWN, SLOTS), 1)) == iota((OWN, SLOTS), 0)).astype(jnp.float32)
    pick = iota((128, SLOTS), 0) == base + iota((128, SLOTS), 1) % CAP
    return jnp.sum(jnp.where(pick, exact_dot(table.T, spread), 0.0), axis=0, keepdims=True)


def kernel(
    emb, cl_in, ord_in, out_ref,
    x_vm, cl_ref, ord_ref, send, recv, recv2, unit_q, unit_k, code_s, code_r, code_r2, res_s, res_r, own_code, code_tmp, far_code,
    in_sem, pay_s, pay_r, code_ss, code_rs, res_ss, res_rs, fwd_s, fwd_r, cfwd_s, cfwd_r,
):
    rep, me = lax.axis_index("rep"), lax.axis_index("own")
    my_z, my_x, my_y = me // PLANE, me // NY % NX, me % NY
    other = 1 - rep
    base = (me % 32) * CAP
    z_at = [(my_z + d) % NZ for d in range(NZ)]
    x_at = [(my_x + d) % NX for d in range(NX)]
    y_at = [(my_y + d) % NY for d in range(NY)]
    z_row = [z * PLANE for z in z_at]
    in_plane = [x_at[dx] * NY + y_at[dy] for dx, dy in PLANE_ORDER]

    def peers(dz):
        return [z_row[dz] + p for p in (in_plane[:-1] if dz == 0 else in_plane)]

    def push(src, dst, send_sem, recv_sem, to, core=rep):
        copy = pltpu.make_async_remote_copy(
            src_ref=src, dst_ref=dst, send_sem=send_sem, recv_sem=recv_sem, device_id=(core, to), device_id_type=MESH
        )
        copy.start()
        return copy

    def landed(ref, n, sem):
        part = ref.at[pl.ds(0, n)]
        pltpu.make_async_copy(part, part, sem).wait()

    barrier = pltpu.get_barrier_semaphore()
    for dz in Z_ORDER:
        for to in peers(dz):
            pl.semaphore_signal(barrier, inc=1, device_id=(rep, to), device_id_type=MESH)
    pl.semaphore_signal(barrier, inc=1, device_id=(other, me), device_id_type=MESH)
    loads = [
        pltpu.make_async_copy(src, dst, in_sem.at[i])
        for i, (src, dst) in enumerate(((cl_in, cl_ref), (ord_in, ord_ref), (emb, x_vm)))
    ]
    for load in loads:
        load.start()
    for load in loads[:2]:
        load.wait()

    cl_row, ord_row = cl_ref[...], ord_ref[...]
    square = (ROWS, ROWS)
    eye = iota(square, 0) == iota(square, 1)
    own_row = cl_row // CL_DEV
    own_col = column_of(own_row, eye)
    earlier = (own_col == own_row) & (iota(square, 0) < iota(square, 1))
    slot_row = jnp.sum(earlier.astype(jnp.int32), axis=0, keepdims=True)
    placed_row = own_row * CAP + slot_row
    code_row = (cl_row % CL_DEV) * 65536 + ord_row
    placed_col = column_of(placed_row, eye)
    code_col = column_of(code_row, eye)
    sent = placed_col == iota((ROWS, SLOTS), 1)
    codes = jnp.sum(jnp.where(sent, code_col + 1, 0), axis=0, keepdims=True) - 1
    for c in range(4):
        code_s[c] = codes[:, 128 * c : 128 * c + 128]

    loads[2].wait()
    values = x_vm[...].astype(jnp.float32)
    scale = lax.rsqrt(jnp.sum(values * values, axis=1, keepdims=True) + 1e-06)
    unit = (values * scale).astype(jnp.bfloat16)
    place = (iota((SLOTS, ROWS), 0) == placed_row).astype(jnp.bfloat16)
    low = iota((1, 8, WIDE), 1) < CAP
    evens, odds = [], []
    for half in range(2):
        first, second = (
            jnp.dot(place, unit[:, q * WIDE : (q + 1) * WIDE], preferred_element_type=jnp.float32).reshape(
                OWN // 2, 8, WIDE
            )
            for q in (2 * half, 2 * half + 1)
        )
        evens.append(jnp.where(low, first, jnp.roll(second, CAP, axis=1)))
        odds.append(jnp.where(low, jnp.roll(first, CAP, axis=1), second))
    packed = jnp.stack([jnp.stack(evens, axis=1), jnp.stack(odds, axis=1)], axis=1)
    send[...] = packed.reshape(OWN * MSG, WIDE).astype(jnp.bfloat16)

    pl.semaphore_wait(barrier, OWN)

    def push_blocks(dz):
        mine = recv.at[pl.ds(pl.multiple_of(me * MSG, MSG), MSG)]
        for to in peers(dz):
            push(send.at[pl.ds(pl.multiple_of(to * MSG, MSG), MSG)], mine, pay_s, pay_r.at[dz], to)

    for dz in range(1, NZ):
        push(code_s.at[z_at[dz] // 2], code_r.at[my_y, my_x, my_z], code_ss.at[0], code_rs.at[0], me - my_z * PLANE + z_row[dz])
    push_blocks(Z_ORDER[0])
    code_r[my_y, my_x, my_z] = code_s[my_z // 2]
    landed(code_r.at[0, 0], NZ - 1, code_rs.at[0])
    for dx in range(1, NX):
        line = code_r.at[my_y, my_x]
        push(line, line, code_ss.at[1], code_rs.at[1], me + (x_at[dx] - my_x) * NY)
    for dz in Z_ORDER[1:3]:
        push_blocks(dz)
    landed(code_r.at[0], NX - 1, code_rs.at[1])
    for dy in range(1, NY):
        line = code_r.at[my_y]
        push(line, line, code_ss.at[2], code_rs.at[2], me + y_at[dy] - my_y)
    for dz in Z_ORDER[3:]:
        push_blocks(dz)

    mine = pl.ds(pl.multiple_of(me * MSG, MSG), MSG)
    recv[mine, :] = send[mine, :]
    landed(code_r, NY - 1, code_rs.at[2])
    code_forward = push(code_r, code_r2, cfwd_s, cfwd_r, me, other)
    table = code_r[...].reshape(OWN, 128).astype(jnp.float32)
    own_code[...] = slot_column(table, base)
    query_row = slot_row_of(table, base)
    query_low = jnp.floor(query_row * (1.0 / 65536)) * 65536
    code_forward.wait()
    code_tmp[...] = slot_column(code_r2[...].reshape(OWN, 128).astype(jnp.float32), base)
    landed(code_r.at[0, 0], NZ - 1, code_ss.at[0])
    landed(code_r.at[0], NX - 1, code_ss.at[1])
    landed(code_r, NY - 1, code_ss.at[2])

    forwards = []
    for i, dz in enumerate(Z_ORDER):
        z = z_at[(NZ - dz) % NZ]
        start = pl.multiple_of(z * GROUP, GROUP)
        slots = pl.ds(pl.multiple_of(z * TILE, TILE), TILE)
        far_code[pl.ds(i * TILE, TILE), :] = code_tmp[slots, :]
        landed(recv, GROUP - (MSG if dz == 0 else 0), pay_r.at[dz])
        block = pl.ds(start, GROUP)
        forwards.append((push(recv.at[block], recv2.at[block], fwd_s.at[dz], fwd_r.at[dz], me, other), start))
        unpack_group(recv, unit_q, start, pl.multiple_of(z * TILE, TILE))

    def best_of(best, keys, code, first, count):
        similar = lax.dot_general(
            keys[pl.ds(first, count), :], unit_q[...], (((1,), (1,)), ((), ())), preferred_element_type=jnp.float32
        )
        at = code[pl.ds(first, count), 0:1]
        allowed = (at >= query_low) & (at < query_row)
        similar = jnp.where(allowed, similar, -1.0).reshape(count // 8, 8, SLOTS)
        return jnp.maximum(best, jnp.max(similar, axis=0))

    best = jnp.full((8, SLOTS), -1.0, jnp.float32)
    for first in (0, 256):
        best = best_of(best, unit_q, own_code, first, 256)
    for i, (forward, start) in enumerate(forwards):
        forward.wait()
        unpack_group(recv2, unit_k, start, i * TILE)
        if i == 3:
            best = best_of(best, unit_k, far_code, 0, 256)
        if i == 6:
            best = best_of(best, unit_k, far_code, 256, 192)
    best = best_of(best, unit_k, far_code, SLOTS - TILE, TILE)
    best = jnp.max(best, axis=0, keepdims=True)
    for c in range(4):
        res_s[c] = best[:, 128 * c : 128 * c + 128]

    for dz in Z_ORDER:
        chunk = res_s.at[z_at[dz] // 2]
        for to in peers(dz):
            push(chunk, res_r.at[me], res_ss, res_rs, to)
    res_r[me] = res_s[my_z // 2]
    landed(send, (OWN - 1) * MSG, pay_s)
    landed(res_r, OWN - 1, res_ss)
    landed(res_r, OWN - 1, res_rs)

    home = res_r[...].reshape(OWN, 128)
    lane = iota((OWN, 128), 1)
    owner_here = iota((OWN, ROWS), 0) == own_row
    nearest = jnp.zeros((OWN, ROWS), jnp.float32)
    for s in range(CAP):
        value = jnp.sum(jnp.where(lane == base + s, home, 0.0), axis=1, keepdims=True)
        nearest = jnp.where(owner_here & (slot_row == s), value, nearest)
    out_ref[...] = jnp.sum(nearest, axis=0, keepdims=True)


def body(embeddings, cluster, order):
    hbm = pl.BlockSpec(memory_space=pl.ANY)
    dma = pltpu.SemaphoreType.DMA
    blocks = pltpu.VMEM((OWN * MSG, WIDE), jnp.bfloat16)
    units = pltpu.VMEM((SLOTS, D), jnp.bfloat16)
    line = pltpu.VMEM((1, ROWS), jnp.int32)
    table = pltpu.VMEM((NY, NX, NZ, 1, 128), jnp.int32)
    codes = pltpu.VMEM((SLOTS, 128), jnp.float32)
    result = pl.pallas_call(
        kernel,
        out_shape=jax.ShapeDtypeStruct((1, ROWS), jnp.float32),
        in_specs=[hbm, hbm, hbm],
        out_specs=pl.BlockSpec(memory_space=pltpu.VMEM),
        scratch_shapes=[
            pltpu.VMEM((ROWS, D), jnp.bfloat16), line, line, blocks, blocks, blocks, units, units,
            pltpu.VMEM((4, 1, 128), jnp.int32), table, table,
            pltpu.VMEM((4, 1, 128), jnp.float32), pltpu.VMEM((OWN, 1, 128), jnp.float32), codes, codes, codes,
            dma((3,)), dma, dma((NZ,)), dma((3,)), dma((3,)), dma, dma, dma((NZ,)), dma((NZ,)), dma, dma,
        ],
        compiler_params=pltpu.CompilerParams(
            collective_id=0, has_side_effects=True, vmem_limit_bytes=60 * 2**20
        ),
    )(embeddings, cluster.reshape(1, ROWS), order.reshape(1, ROWS))
    return result.reshape(ROWS)


def solution(mesh):
    placed = (P(("rep", "own"), None), P(("rep", "own")), P(("rep", "own")))
    return jax.shard_map(body, mesh=mesh, in_specs=placed, out_specs=P(("rep", "own")), check_vma=False)
```

```python
import jax
import jax.numpy as jnp
from jax import lax
from jax.experimental import pallas as pl
from jax.experimental.pallas import tpu as pltpu
from jax.sharding import PartitionSpec as P

MESH = pl.DeviceIdType.MESH
CL_DEV = 4
CAP = 4
NZ, NX, NY = 8, 4, 4
OWN = NZ * NX * NY
PLANE = NX * NY
ROWS = 256
D = 1024
SLOTS = OWN * CAP
WIDE = D // 4
MSG = 16
GROUP = PLANE * MSG
TILE = PLANE * CAP
Z_ORDER = (4, 3, 5, 2, 6, 1, 7, 0)
LAND_ORDER = (0, 3, 5, 4, 2, 6, 1, 7)
RELAY = 4
PLANE_ORDER = ((2, 2), (2, 1), (1, 2), (2, 3), (3, 2), (1, 1), (3, 3), (1, 3), (3, 1), (2, 0), (0, 2), (1, 0), (0, 1), (3, 0), (0, 3), (0, 0))


def iota(shape, dim):
    return lax.broadcasted_iota(jnp.int32, shape, dim)


def column_of(row, eye):
    return jnp.sum(jnp.where(eye, row, 0), axis=1, keepdims=True)


def exact_dot(a, b):
    return jnp.dot(a, b, precision=lax.Precision.HIGHEST, preferred_element_type=jnp.float32)


def unpack_group(src, dst, src_row, dst_row):
    block = src[pl.ds(src_row, GROUP), :].astype(jnp.float32).reshape(PLANE // 2, 2, 2, 8, WIDE)
    low = iota((1, 8, WIDE), 1) < CAP
    for half in range(2):
        even, odd = block[:, 0, half], block[:, 1, half]
        first = jnp.where(low, even, jnp.roll(odd, CAP, axis=1))
        second = jnp.where(low, jnp.roll(even, CAP, axis=1), odd)
        for i, part in enumerate((first, second)):
            lane = (2 * half + i) * WIDE
            dst[pl.ds(dst_row, TILE), lane : lane + WIDE] = part.reshape(TILE, WIDE).astype(jnp.bfloat16)


def source_row(slot):
    source = slot // CAP
    return (source % NY * NX + source // NY % NX) * NZ + source // PLANE


def slot_column(table, base):
    spread = (source_row(iota((SLOTS, OWN), 0)) == iota((SLOTS, OWN), 1)).astype(jnp.float32)
    pick = iota((SLOTS, 128), 1) == base + iota((SLOTS, 128), 0) % CAP
    column = jnp.sum(jnp.where(pick, exact_dot(spread, table), 0.0), axis=1, keepdims=True)
    return jnp.broadcast_to(column, (SLOTS, 128))


def slot_row_of(table, base):
    spread = (source_row(iota((OWN, SLOTS), 1)) == iota((OWN, SLOTS), 0)).astype(jnp.float32)
    pick = iota((128, SLOTS), 0) == base + iota((128, SLOTS), 1) % CAP
    return jnp.sum(jnp.where(pick, exact_dot(table.T, spread), 0.0), axis=0, keepdims=True)


def kernel(
    emb, cl_in, ord_in, out_ref,
    x_vm, cl_ref, ord_ref, send, recv, recv2, relay, unit_q, unit_k, code_s, code_r, code_r2, res_s, res_r, own_code, code_tmp, far_code,
    in_sem, pay_s, pay_r, code_ss, code_rs, res_ss, res_rs, fwd_s, fwd_r, cfwd_s, cfwd_r, relay_s, relay_r, ready,
):
    rep, me = lax.axis_index("rep"), lax.axis_index("own")
    my_z, my_x, my_y = me // PLANE, me // NY % NX, me % NY
    other = 1 - rep
    base = (me % 32) * CAP
    z_at = [(my_z + d) % NZ for d in range(NZ)]
    x_at = [(my_x + d) % NX for d in range(NX)]
    y_at = [(my_y + d) % NY for d in range(NY)]
    z_row = [z * PLANE for z in z_at]
    in_plane = [x_at[dx] * NY + y_at[dy] for dx, dy in PLANE_ORDER]

    def peers(dz):
        return [z_row[dz] + p for p in (in_plane[:-1] if dz == 0 else in_plane)]

    def push(src, dst, send_sem, recv_sem, to, core=rep):
        copy = pltpu.make_async_remote_copy(
            src_ref=src, dst_ref=dst, send_sem=send_sem, recv_sem=recv_sem, device_id=(core, to), device_id_type=MESH
        )
        copy.start()
        return copy

    def landed(ref, n, sem):
        part = ref.at[pl.ds(0, n)]
        pltpu.make_async_copy(part, part, sem).wait()

    barrier = pltpu.get_barrier_semaphore()
    column = me - my_z * PLANE
    line = [column + z_row[dz] for dz in range(NZ)]
    near = [line[dz] for dz in Z_ORDER[:-1]] + peers(0)
    for to in near:
        pl.semaphore_signal(barrier, inc=1, device_id=(rep, to), device_id_type=MESH)
    pl.semaphore_signal(barrier, inc=1, device_id=(other, me), device_id_type=MESH)
    loads = [
        pltpu.make_async_copy(src, dst, in_sem.at[i])
        for i, (src, dst) in enumerate(((cl_in, cl_ref), (ord_in, ord_ref), (emb, x_vm)))
    ]
    for load in loads:
        load.start()
    for load in loads[:2]:
        load.wait()

    cl_row, ord_row = cl_ref[...], ord_ref[...]
    square = (ROWS, ROWS)
    eye = iota(square, 0) == iota(square, 1)
    own_row = cl_row // CL_DEV
    own_col = column_of(own_row, eye)
    earlier = (own_col == own_row) & (iota(square, 0) < iota(square, 1))
    slot_row = jnp.sum(earlier.astype(jnp.int32), axis=0, keepdims=True)
    placed_row = own_row * CAP + slot_row
    code_row = (cl_row % CL_DEV) * 65536 + ord_row
    placed_col = column_of(placed_row, eye)
    code_col = column_of(code_row, eye)
    sent = placed_col == iota((ROWS, SLOTS), 1)
    codes = jnp.sum(jnp.where(sent, code_col + 1, 0), axis=0, keepdims=True) - 1
    for c in range(4):
        code_s[c] = codes[:, 128 * c : 128 * c + 128]

    loads[2].wait()
    values = x_vm[...].astype(jnp.float32)
    scale = lax.rsqrt(jnp.sum(values * values, axis=1, keepdims=True) + 1e-06)
    unit = (values * scale).astype(jnp.bfloat16)
    place = (iota((SLOTS, ROWS), 0) == placed_row).astype(jnp.bfloat16)
    low = iota((1, 8, WIDE), 1) < CAP
    evens, odds = [], []
    for half in range(2):
        first, second = (
            jnp.dot(place, unit[:, q * WIDE : (q + 1) * WIDE], preferred_element_type=jnp.float32).reshape(
                OWN // 2, 8, WIDE
            )
            for q in (2 * half, 2 * half + 1)
        )
        evens.append(jnp.where(low, first, jnp.roll(second, CAP, axis=1)))
        odds.append(jnp.where(low, jnp.roll(first, CAP, axis=1), second))
    packed = jnp.stack([jnp.stack(evens, axis=1), jnp.stack(odds, axis=1)], axis=1)
    send[...] = packed.reshape(OWN * MSG, WIDE).astype(jnp.bfloat16)

    def block_of(ref, index):
        return ref.at[pl.ds(pl.multiple_of(index * MSG, MSG), MSG)]

    def push_blocks(*groups):
        for pair in zip(*(peers(dz) for dz in groups)):
            for dz, to in zip(groups, pair):
                push(block_of(send, to), block_of(recv, me), pay_s, pay_r.at[dz], to)

    pl.semaphore_wait(barrier, len(near) + 1)
    for to in peers(0):
        pl.semaphore_signal(ready, inc=1, device_id=(rep, to), device_id_type=MESH)

    for dz in Z_ORDER[:-1]:
        push(code_s.at[z_at[dz] // 2], code_r.at[my_y, my_x, my_z], code_ss.at[0], code_rs.at[0], line[dz])
    opposite = send.at[pl.ds(pl.multiple_of(z_at[RELAY] * GROUP, GROUP), GROUP)]
    relayed = push(opposite, relay, relay_s, relay_r, line[RELAY])
    push_blocks(0)
    pl.semaphore_wait(ready, PLANE - 1)
    push_blocks(3, 5)
    code_r[my_y, my_x, my_z] = code_s[my_z // 2]
    landed(code_r.at[0, 0], NZ - 1, code_rs.at[0])
    for dx in range(1, NX):
        part = code_r.at[my_y, my_x]
        push(part, part, code_ss.at[1], code_rs.at[1], me + (x_at[dx] - my_x) * NY)
    relayed.wait()
    source = line[RELAY]
    for p, to in zip(in_plane, peers(0)):
        push(block_of(relay, p), block_of(recv, source), pay_s, pay_r.at[RELAY], to)
    push_blocks(2, 6)
    landed(code_r.at[0], NX - 1, code_rs.at[1])
    for dy in range(1, NY):
        part = code_r.at[my_y]
        push(part, part, code_ss.at[2], code_rs.at[2], me + y_at[dy] - my_y)
    push_blocks(1, 7)

    handed = pl.ds(pl.multiple_of(source * MSG, MSG), MSG)
    recv[handed, :] = relay[pl.ds(pl.multiple_of(in_plane[-1] * MSG, MSG), MSG), :]
    mine = pl.ds(pl.multiple_of(me * MSG, MSG), MSG)
    recv[mine, :] = send[mine, :]
    landed(code_r, NY - 1, code_rs.at[2])
    code_forward = push(code_r, code_r2, cfwd_s, cfwd_r, me, other)
    table = code_r[...].reshape(OWN, 128).astype(jnp.float32)
    own_code[...] = slot_column(table, base)
    query_row = slot_row_of(table, base)
    query_low = jnp.floor(query_row * (1.0 / 65536)) * 65536
    code_forward.wait()
    code_tmp[...] = slot_column(code_r2[...].reshape(OWN, 128).astype(jnp.float32), base)
    landed(code_r.at[0, 0], NZ - 1, code_ss.at[0])
    landed(code_r.at[0], NX - 1, code_ss.at[1])
    landed(code_r, NY - 1, code_ss.at[2])

    forwards = []
    for i, dz in enumerate(LAND_ORDER):
        z = z_at[(NZ - dz) % NZ]
        start = pl.multiple_of(z * GROUP, GROUP)
        slots = pl.ds(pl.multiple_of(z * TILE, TILE), TILE)
        far_code[pl.ds(i * TILE, TILE), :] = code_tmp[slots, :]
        landed(recv, GROUP - (MSG if dz in (0, RELAY) else 0), pay_r.at[dz])
        block = pl.ds(start, GROUP)
        forwards.append((push(recv.at[block], recv2.at[block], fwd_s.at[dz], fwd_r.at[dz], me, other), start))
        unpack_group(recv, unit_q, start, pl.multiple_of(z * TILE, TILE))

    def best_of(best, keys, code, first, count):
        similar = lax.dot_general(
            keys[pl.ds(first, count), :], unit_q[...], (((1,), (1,)), ((), ())), preferred_element_type=jnp.float32
        )
        at = code[pl.ds(first, count), 0:1]
        allowed = (at >= query_low) & (at < query_row)
        similar = jnp.where(allowed, similar, -1.0).reshape(count // 8, 8, SLOTS)
        return jnp.maximum(best, jnp.max(similar, axis=0))

    best = jnp.full((8, SLOTS), -1.0, jnp.float32)
    for first in (0, 256):
        best = best_of(best, unit_q, own_code, first, 256)
    for i, (forward, start) in enumerate(forwards):
        forward.wait()
        unpack_group(recv2, unit_k, start, i * TILE)
        if i == 3:
            best = best_of(best, unit_k, far_code, 0, 256)
        if i == 6:
            best = best_of(best, unit_k, far_code, 256, 192)
    best = best_of(best, unit_k, far_code, SLOTS - TILE, TILE)
    best = jnp.max(best, axis=0, keepdims=True)
    for c in range(4):
        res_s[c] = best[:, 128 * c : 128 * c + 128]

    for dz in Z_ORDER:
        chunk = res_s.at[z_at[dz] // 2]
        for to in peers(dz):
            push(chunk, res_r.at[me], res_ss, res_rs, to)
    res_r[me] = res_s[my_z // 2]
    landed(send, (OWN - 2) * MSG, pay_s)
    landed(res_r, OWN - 1, res_ss)
    landed(res_r, OWN - 1, res_rs)

    home = res_r[...].reshape(OWN, 128)
    lane = iota((OWN, 128), 1)
    owner_here = iota((OWN, ROWS), 0) == own_row
    nearest = jnp.zeros((OWN, ROWS), jnp.float32)
    for s in range(CAP):
        value = jnp.sum(jnp.where(lane == base + s, home, 0.0), axis=1, keepdims=True)
        nearest = jnp.where(owner_here & (slot_row == s), value, nearest)
    out_ref[...] = jnp.sum(nearest, axis=0, keepdims=True)


def body(embeddings, cluster, order):
    hbm = pl.BlockSpec(memory_space=pl.ANY)
    dma = pltpu.SemaphoreType.DMA
    blocks = pltpu.VMEM((OWN * MSG, WIDE), jnp.bfloat16)
    units = pltpu.VMEM((SLOTS, D), jnp.bfloat16)
    line = pltpu.VMEM((1, ROWS), jnp.int32)
    table = pltpu.VMEM((NY, NX, NZ, 1, 128), jnp.int32)
    codes = pltpu.VMEM((SLOTS, 128), jnp.float32)
    result = pl.pallas_call(
        kernel,
        out_shape=jax.ShapeDtypeStruct((1, ROWS), jnp.float32),
        in_specs=[hbm, hbm, hbm],
        out_specs=pl.BlockSpec(memory_space=pltpu.VMEM),
        scratch_shapes=[
            pltpu.VMEM((ROWS, D), jnp.bfloat16), line, line, blocks, blocks, blocks,
            pltpu.VMEM((GROUP, WIDE), jnp.bfloat16), units, units,
            pltpu.VMEM((4, 1, 128), jnp.int32), table, table,
            pltpu.VMEM((4, 1, 128), jnp.float32), pltpu.VMEM((OWN, 1, 128), jnp.float32), codes, codes, codes,
            dma((3,)), dma, dma((NZ,)), dma((3,)), dma((3,)), dma, dma, dma((NZ,)), dma((NZ,)), dma, dma, dma, dma,
            pltpu.SemaphoreType.REGULAR,
        ],
        compiler_params=pltpu.CompilerParams(
            collective_id=0, has_side_effects=True, vmem_limit_bytes=60 * 2**20
        ),
    )(embeddings, cluster.reshape(1, ROWS), order.reshape(1, ROWS))
    return jnp.maximum(result.reshape(ROWS), -1.0)


def solution(mesh):
    placed = (P(("rep", "own"), None), P(("rep", "own")), P(("rep", "own")))
    return jax.shard_map(body, mesh=mesh, in_specs=placed, out_specs=P(("rep", "own")), check_vma=False)
```

```python
import jax
import jax.numpy as jnp
from jax import lax
from jax.experimental import pallas as pl
from jax.experimental.pallas import tpu as pltpu
from jax.sharding import PartitionSpec as P

MESH = pl.DeviceIdType.MESH
CL_DEV = 4
CAP = 4
NZ, NX, NY = 8, 4, 4
OWN = NZ * NX * NY
PLANE = NX * NY
ROWS = 256
D = 1024
SLOTS = OWN * CAP
WIDE = D // 4
MSG = 16
GROUP = PLANE * MSG
TILE = PLANE * CAP
Z_ORDER = (4, 3, 5, 2, 6, 1, 7, 0)
LAND_ORDER = (0, 1, 7, 3, 5, 4, 2, 6)
RELAYS = (1, 7, 4)
VMEM_BYTES = 55226 * 2**10
PLANE_ORDER = ((2, 2), (2, 1), (1, 2), (2, 3), (3, 2), (1, 1), (3, 3), (1, 3), (3, 1), (2, 0), (0, 2), (1, 0), (0, 1), (3, 0), (0, 3), (0, 0))


def iota(shape, dim):
    return lax.broadcasted_iota(jnp.int32, shape, dim)


def column_of(row, eye):
    return jnp.sum(jnp.where(eye, row, 0), axis=1, keepdims=True)


def exact_dot(a, b):
    return jnp.dot(a, b, precision=lax.Precision.HIGHEST, preferred_element_type=jnp.float32)


def unpack_group(src, dst, src_row, dst_row):
    block = src[pl.ds(src_row, GROUP), :].astype(jnp.float32).reshape(PLANE // 2, 2, 2, 8, WIDE)
    low = iota((1, 8, WIDE), 1) < CAP
    for half in range(2):
        even, odd = block[:, 0, half], block[:, 1, half]
        first = jnp.where(low, even, jnp.roll(odd, CAP, axis=1))
        second = jnp.where(low, jnp.roll(even, CAP, axis=1), odd)
        for i, part in enumerate((first, second)):
            lane = (2 * half + i) * WIDE
            dst[pl.ds(dst_row, TILE), lane : lane + WIDE] = part.reshape(TILE, WIDE).astype(jnp.bfloat16)


def source_row(slot):
    source = slot // CAP
    return (source % NY * NX + source // NY % NX) * NZ + source // PLANE


def slot_column(table, base):
    spread = (source_row(iota((SLOTS, OWN), 0)) == iota((SLOTS, OWN), 1)).astype(jnp.float32)
    pick = iota((SLOTS, 128), 1) == base + iota((SLOTS, 128), 0) % CAP
    column = jnp.sum(jnp.where(pick, exact_dot(spread, table), 0.0), axis=1, keepdims=True)
    return jnp.broadcast_to(column, (SLOTS, 128))


def slot_row_of(table, base):
    spread = (source_row(iota((OWN, SLOTS), 1)) == iota((OWN, SLOTS), 0)).astype(jnp.float32)
    pick = iota((128, SLOTS), 0) == base + iota((128, SLOTS), 1) % CAP
    return jnp.sum(jnp.where(pick, exact_dot(table.T, spread), 0.0), axis=0, keepdims=True)


def kernel(
    emb, cl_in, ord_in, out_ref,
    x_vm, cl_ref, ord_ref, send, recv, recv2, relay, unit_q, unit_k, code_s, code_r, code_r2, res_s, res_r, own_code, code_tmp, far_code,
    in_sem, pay_s, pay_r, code_ss, code_rs, res_ss, res_rs, fwd_s, fwd_r, cfwd_s, cfwd_r, relay_s, relay_r, ready,
):
    rep, me = lax.axis_index("rep"), lax.axis_index("own")
    my_z, my_x, my_y = me // PLANE, me // NY % NX, me % NY
    other = 1 - rep
    base = (me % 32) * CAP
    z_at = [(my_z + d) % NZ for d in range(NZ)]
    x_at = [(my_x + d) % NX for d in range(NX)]
    y_at = [(my_y + d) % NY for d in range(NY)]
    z_row = [z * PLANE for z in z_at]
    in_plane = [x_at[dx] * NY + y_at[dy] for dx, dy in PLANE_ORDER]

    def peers(dz):
        return [z_row[dz] + p for p in (in_plane[:-1] if dz == 0 else in_plane)]

    def push(src, dst, send_sem, recv_sem, to, core=rep):
        copy = pltpu.make_async_remote_copy(
            src_ref=src, dst_ref=dst, send_sem=send_sem, recv_sem=recv_sem, device_id=(core, to), device_id_type=MESH
        )
        copy.start()
        return copy

    def landed(ref, n, sem):
        part = ref.at[pl.ds(0, n)]
        pltpu.make_async_copy(part, part, sem).wait()

    barrier = pltpu.get_barrier_semaphore()
    column = me - my_z * PLANE
    line = [column + z_row[dz] for dz in range(NZ)]
    near = [line[dz] for dz in Z_ORDER[:-1]] + peers(0)
    for to in near:
        pl.semaphore_signal(barrier, inc=1, device_id=(rep, to), device_id_type=MESH)
    pl.semaphore_signal(barrier, inc=1, device_id=(other, me), device_id_type=MESH)
    loads = [
        pltpu.make_async_copy(src, dst, in_sem.at[i])
        for i, (src, dst) in enumerate(((cl_in, cl_ref), (ord_in, ord_ref), (emb, x_vm)))
    ]
    for load in loads:
        load.start()
    for load in loads[:2]:
        load.wait()

    cl_row, ord_row = cl_ref[...], ord_ref[...]
    square = (ROWS, ROWS)
    eye = iota(square, 0) == iota(square, 1)
    own_row = cl_row // CL_DEV
    own_col = column_of(own_row, eye)
    earlier = (own_col == own_row) & (iota(square, 0) < iota(square, 1))
    slot_row = jnp.sum(earlier.astype(jnp.int32), axis=0, keepdims=True)
    placed_row = own_row * CAP + slot_row
    code_row = (cl_row % CL_DEV) * 65536 + ord_row
    placed_col = column_of(placed_row, eye)
    code_col = column_of(code_row, eye)
    sent = placed_col == iota((ROWS, SLOTS), 1)
    codes = jnp.sum(jnp.where(sent, code_col + 1, 0), axis=0, keepdims=True) - 1
    for c in range(4):
        code_s[c] = codes[:, 128 * c : 128 * c + 128]

    loads[2].wait()
    values = x_vm[...].astype(jnp.float32)
    scale = lax.rsqrt(jnp.sum(values * values, axis=1, keepdims=True) + 1e-06)
    unit = (values * scale).astype(jnp.bfloat16)
    place = (iota((SLOTS, ROWS), 0) == placed_row).astype(jnp.bfloat16)
    low = iota((1, 8, WIDE), 1) < CAP
    evens, odds = [], []
    for half in range(2):
        first, second = (
            jnp.dot(place, unit[:, q * WIDE : (q + 1) * WIDE], preferred_element_type=jnp.float32).reshape(
                OWN // 2, 8, WIDE
            )
            for q in (2 * half, 2 * half + 1)
        )
        evens.append(jnp.where(low, first, jnp.roll(second, CAP, axis=1)))
        odds.append(jnp.where(low, jnp.roll(first, CAP, axis=1), second))
    packed = jnp.stack([jnp.stack(evens, axis=1), jnp.stack(odds, axis=1)], axis=1)
    send[...] = packed.reshape(OWN * MSG, WIDE).astype(jnp.bfloat16)

    def block_of(ref, index):
        return ref.at[pl.ds(pl.multiple_of(index * MSG, MSG), MSG)]

    def push_blocks(*groups):
        for pair in zip(*(peers(dz) for dz in groups)):
            for dz, to in zip(groups, pair):
                push(block_of(send, to), block_of(recv, me), pay_s, pay_r.at[dz], to)

    pl.semaphore_wait(barrier, len(near) + 1)
    for to in peers(0):
        pl.semaphore_signal(ready, inc=1, device_id=(rep, to), device_id_type=MESH)

    for dz in Z_ORDER[:-1]:
        push(code_s.at[z_at[dz] // 2], code_r.at[my_y, my_x, my_z], code_ss.at[0], code_rs.at[0], line[dz])
    blocks = [
        push(
            send.at[pl.ds(pl.multiple_of(z_at[dz] * GROUP, GROUP), GROUP)], relay.at[pl.ds(i * GROUP, GROUP)],
            relay_s.at[i], relay_r.at[i], line[dz],
        )
        for i, dz in enumerate(RELAYS)
    ]

    def hand_on(i):
        blocks[i].wait()
        source = line[(NZ - RELAYS[i]) % NZ]
        for p, to in zip(in_plane, peers(0)):
            push(block_of(relay, i * PLANE + p), block_of(recv, source), pay_s, pay_r.at[RELAYS[i]], to)
        kept = pl.ds(pl.multiple_of(i * GROUP + in_plane[-1] * MSG, MSG), MSG)
        recv[pl.ds(pl.multiple_of(source * MSG, MSG), MSG), :] = relay[kept, :]

    push_blocks(0)
    pl.semaphore_wait(ready, PLANE - 1)
    push_blocks(3, 5)
    code_r[my_y, my_x, my_z] = code_s[my_z // 2]
    landed(code_r.at[0, 0], NZ - 1, code_rs.at[0])
    for dx in range(1, NX):
        part = code_r.at[my_y, my_x]
        push(part, part, code_ss.at[1], code_rs.at[1], me + (x_at[dx] - my_x) * NY)
    hand_on(0)
    hand_on(1)
    landed(code_r.at[0], NX - 1, code_rs.at[1])
    for dy in range(1, NY):
        part = code_r.at[my_y]
        push(part, part, code_ss.at[2], code_rs.at[2], me + y_at[dy] - my_y)
    hand_on(2)
    push_blocks(2, 6)

    mine = pl.ds(pl.multiple_of(me * MSG, MSG), MSG)
    recv[mine, :] = send[mine, :]
    landed(code_r, NY - 1, code_rs.at[2])
    code_forward = push(code_r, code_r2, cfwd_s, cfwd_r, me, other)
    table = code_r[...].reshape(OWN, 128).astype(jnp.float32)
    own_code[...] = slot_column(table, base)
    query_row = slot_row_of(table, base)
    query_low = jnp.floor(query_row * (1.0 / 65536)) * 65536
    code_forward.wait()
    code_tmp[...] = slot_column(code_r2[...].reshape(OWN, 128).astype(jnp.float32), base)
    landed(code_r.at[0, 0], NZ - 1, code_ss.at[0])
    landed(code_r.at[0], NX - 1, code_ss.at[1])
    landed(code_r, NY - 1, code_ss.at[2])

    forwards = []
    for i, dz in enumerate(LAND_ORDER):
        z = z_at[(NZ - dz) % NZ]
        start = pl.multiple_of(z * GROUP, GROUP)
        slots = pl.ds(pl.multiple_of(z * TILE, TILE), TILE)
        far_code[pl.ds(i * TILE, TILE), :] = code_tmp[slots, :]
        landed(recv, GROUP - (MSG if dz in (0, *RELAYS) else 0), pay_r.at[dz])
        block = pl.ds(start, GROUP)
        forwards.append((push(recv.at[block], recv2.at[block], fwd_s.at[dz], fwd_r.at[dz], me, other), start))
        unpack_group(recv, unit_q, start, pl.multiple_of(z * TILE, TILE))

    def best_of(best, keys, code, first, count):
        similar = lax.dot_general(
            keys[pl.ds(first, count), :], unit_q[...], (((1,), (1,)), ((), ())), preferred_element_type=jnp.float32
        )
        at = code[pl.ds(first, count), 0:1]
        allowed = (at >= query_low) & (at < query_row)
        similar = jnp.where(allowed, similar, -1.0).reshape(count // 8, 8, SLOTS)
        return jnp.maximum(best, jnp.max(similar, axis=0))

    best = jnp.full((8, SLOTS), -1.0, jnp.float32)
    for first in (0, 256):
        best = best_of(best, unit_q, own_code, first, 256)
    for i, (forward, start) in enumerate(forwards):
        forward.wait()
        unpack_group(recv2, unit_k, start, i * TILE)
        if i == 3:
            best = best_of(best, unit_k, far_code, 0, 256)
        if i == 6:
            best = best_of(best, unit_k, far_code, 256, 192)
    best = best_of(best, unit_k, far_code, SLOTS - TILE, TILE)
    best = jnp.max(best, axis=0, keepdims=True)
    for c in range(4):
        res_s[c] = best[:, 128 * c : 128 * c + 128]

    for dz in Z_ORDER:
        chunk = res_s.at[z_at[dz] // 2]
        for to in peers(dz):
            push(chunk, res_r.at[me], res_ss, res_rs, to)
    res_r[me] = res_s[my_z // 2]
    landed(send, (OWN - 1 - len(RELAYS)) * MSG, pay_s)
    landed(res_r, OWN - 1, res_ss)
    landed(res_r, OWN - 1, res_rs)

    home = res_r[...].reshape(OWN, 128)
    lane = iota((OWN, 128), 1)
    owner_here = iota((OWN, ROWS), 0) == own_row
    nearest = jnp.zeros((OWN, ROWS), jnp.float32)
    for s in range(CAP):
        value = jnp.sum(jnp.where(lane == base + s, home, 0.0), axis=1, keepdims=True)
        nearest = jnp.where(owner_here & (slot_row == s), value, nearest)
    out_ref[...] = jnp.sum(nearest, axis=0, keepdims=True)


def body(embeddings, cluster, order):
    hbm = pl.BlockSpec(memory_space=pl.ANY)
    dma = pltpu.SemaphoreType.DMA
    blocks = pltpu.VMEM((OWN * MSG, WIDE), jnp.bfloat16)
    units = pltpu.VMEM((SLOTS, D), jnp.bfloat16)
    line = pltpu.VMEM((1, ROWS), jnp.int32)
    table = pltpu.VMEM((NY, NX, NZ, 1, 128), jnp.int32)
    codes = pltpu.VMEM((SLOTS, 128), jnp.float32)
    result = pl.pallas_call(
        kernel,
        out_shape=jax.ShapeDtypeStruct((1, ROWS), jnp.float32),
        in_specs=[hbm, hbm, hbm],
        out_specs=pl.BlockSpec(memory_space=pltpu.VMEM),
        scratch_shapes=[
            pltpu.VMEM((ROWS, D), jnp.bfloat16), line, line, blocks, blocks, blocks,
            pltpu.VMEM((len(RELAYS) * GROUP, WIDE), jnp.bfloat16), units, units,
            pltpu.VMEM((4, 1, 128), jnp.int32), table, table,
            pltpu.VMEM((4, 1, 128), jnp.float32), pltpu.VMEM((OWN, 1, 128), jnp.float32), codes, codes, codes,
            dma((3,)), dma, dma((NZ,)), dma((3,)), dma((3,)), dma, dma, dma((NZ,)), dma((NZ,)), dma, dma,
            dma((len(RELAYS),)), dma((len(RELAYS),)),
            pltpu.SemaphoreType.REGULAR,
        ],
        compiler_params=pltpu.CompilerParams(
            collective_id=0, has_side_effects=True, vmem_limit_bytes=VMEM_BYTES
        ),
    )(embeddings, cluster.reshape(1, ROWS), order.reshape(1, ROWS))
    return result.reshape(ROWS)


def solution(mesh):
    placed = (P(("rep", "own"), None), P(("rep", "own")), P(("rep", "own")))
    return jax.shard_map(body, mesh=mesh, in_specs=placed, out_specs=P(("rep", "own")), check_vma=False)
```

```python
import jax
import jax.numpy as jnp
from jax import lax
from jax.experimental import pallas as pl
from jax.experimental.pallas import tpu as pltpu
from jax.sharding import PartitionSpec as P

MESH = pl.DeviceIdType.MESH
CL_DEV = 4
CAP = 4
NZ, NX, NY = 8, 4, 4
OWN = NZ * NX * NY
PLANE = NX * NY
ROWS = 256
D = 1024
SLOTS = OWN * CAP
WIDE = D // 4
MSG = 16
GROUP = PLANE * MSG
TILE = PLANE * CAP
Z_ORDER = (4, 3, 5, 2, 6, 1, 7, 0)
LAND_ORDER = (0, 2, 6, 3, 5, 4, 1, 7)
RELAYS = (2, 6)
VMEM_BYTES = 55226 * 2**10
PLANE_ORDER = ((2, 2), (2, 1), (1, 2), (2, 3), (3, 2), (1, 1), (3, 3), (1, 3), (3, 1), (2, 0), (0, 2), (1, 0), (0, 1), (3, 0), (0, 3), (0, 0))


def iota(shape, dim):
    return lax.broadcasted_iota(jnp.int32, shape, dim)


def column_of(row, eye):
    return jnp.sum(jnp.where(eye, row, 0), axis=1, keepdims=True)


def exact_dot(a, b):
    return jnp.dot(a, b, precision=lax.Precision.HIGHEST, preferred_element_type=jnp.float32)


def unpack_group(src, dst, src_row, dst_row):
    block = src[pl.ds(src_row, GROUP), :].astype(jnp.float32).reshape(PLANE // 2, 2, 2, 8, WIDE)
    low = iota((1, 8, WIDE), 1) < CAP
    for half in range(2):
        even, odd = block[:, 0, half], block[:, 1, half]
        first = jnp.where(low, even, jnp.roll(odd, CAP, axis=1))
        second = jnp.where(low, jnp.roll(even, CAP, axis=1), odd)
        for i, part in enumerate((first, second)):
            lane = (2 * half + i) * WIDE
            dst[pl.ds(dst_row, TILE), lane : lane + WIDE] = part.reshape(TILE, WIDE).astype(jnp.bfloat16)


def source_row(slot):
    source = slot // CAP
    return (source % NY * NX + source // NY % NX) * NZ + source // PLANE


def slot_column(table, base):
    spread = (source_row(iota((SLOTS, OWN), 0)) == iota((SLOTS, OWN), 1)).astype(jnp.float32)
    pick = iota((SLOTS, 128), 1) == base + iota((SLOTS, 128), 0) % CAP
    column = jnp.sum(jnp.where(pick, exact_dot(spread, table), 0.0), axis=1, keepdims=True)
    return jnp.broadcast_to(column, (SLOTS, 128))


def slot_row_of(table, base):
    spread = (source_row(iota((OWN, SLOTS), 1)) == iota((OWN, SLOTS), 0)).astype(jnp.float32)
    pick = iota((128, SLOTS), 0) == base + iota((128, SLOTS), 1) % CAP
    return jnp.sum(jnp.where(pick, exact_dot(table.T, spread), 0.0), axis=0, keepdims=True)


def kernel(
    emb, cl_in, ord_in, out_ref,
    x_vm, cl_ref, ord_ref, send, recv, recv2, relay, unit_q, unit_k, code_s, code_r, code_r2, res_s, res_r, own_code, code_tmp, far_code,
    in_sem, pay_s, pay_r, code_ss, code_rs, res_ss, res_rs, fwd_s, fwd_r, cfwd_s, cfwd_r, relay_s, relay_r, ready,
):
    rep, me = lax.axis_index("rep"), lax.axis_index("own")
    my_z, my_x, my_y = me // PLANE, me // NY % NX, me % NY
    other = 1 - rep
    base = (me % 32) * CAP
    z_at = [(my_z + d) % NZ for d in range(NZ)]
    x_at = [(my_x + d) % NX for d in range(NX)]
    y_at = [(my_y + d) % NY for d in range(NY)]
    z_row = [z * PLANE for z in z_at]
    in_plane = [x_at[dx] * NY + y_at[dy] for dx, dy in PLANE_ORDER]

    def peers(dz):
        return [z_row[dz] + p for p in (in_plane[:-1] if dz == 0 else in_plane)]

    def push(src, dst, send_sem, recv_sem, to, core=rep):
        copy = pltpu.make_async_remote_copy(
            src_ref=src, dst_ref=dst, send_sem=send_sem, recv_sem=recv_sem, device_id=(core, to), device_id_type=MESH
        )
        copy.start()
        return copy

    def landed(ref, n, sem):
        part = ref.at[pl.ds(0, n)]
        pltpu.make_async_copy(part, part, sem).wait()

    barrier = pltpu.get_barrier_semaphore()
    column = me - my_z * PLANE
    line = [column + z_row[dz] for dz in range(NZ)]
    x_line = [me + (x_at[d] - my_x) * NY for d in range(1, NX)]
    y_line = [me + y_at[d] - my_y for d in range(1, NY)]
    near = [line[dz] for dz in (2, 6, 1, 7)] + x_line + y_line
    for to in near:
        pl.semaphore_signal(barrier, inc=1, device_id=(rep, to), device_id_type=MESH)
    pl.semaphore_signal(barrier, inc=1, device_id=(other, me), device_id_type=MESH)
    loads = [
        pltpu.make_async_copy(src, dst, in_sem.at[i])
        for i, (src, dst) in enumerate(((cl_in, cl_ref), (ord_in, ord_ref), (emb, x_vm)))
    ]
    for load in loads:
        load.start()
    for load in loads[:2]:
        load.wait()

    cl_row, ord_row = cl_ref[...], ord_ref[...]
    square = (ROWS, ROWS)
    eye = iota(square, 0) == iota(square, 1)
    own_row = cl_row // CL_DEV
    own_col = column_of(own_row, eye)
    earlier = (own_col == own_row) & (iota(square, 0) < iota(square, 1))
    slot_row = jnp.sum(earlier.astype(jnp.int32), axis=0, keepdims=True)
    placed_row = own_row * CAP + slot_row
    code_row = (cl_row % CL_DEV) * 65536 + ord_row
    placed_col = column_of(placed_row, eye)
    code_col = column_of(code_row, eye)
    sent = placed_col == iota((ROWS, SLOTS), 1)
    codes = jnp.sum(jnp.where(sent, code_col + 1, 0), axis=0, keepdims=True) - 1
    for c in range(4):
        code_s[c] = codes[:, 128 * c : 128 * c + 128]

    loads[2].wait()
    values = x_vm[...].astype(jnp.float32)
    scale = lax.rsqrt(jnp.sum(values * values, axis=1, keepdims=True) + 1e-06)
    unit = (values * scale).astype(jnp.bfloat16)
    place = (iota((SLOTS, ROWS), 0) == placed_row).astype(jnp.bfloat16)
    low = iota((1, 8, WIDE), 1) < CAP
    evens, odds = [], []
    for half in range(2):
        first, second = (
            jnp.dot(place, unit[:, q * WIDE : (q + 1) * WIDE], preferred_element_type=jnp.float32).reshape(
                OWN // 2, 8, WIDE
            )
            for q in (2 * half, 2 * half + 1)
        )
        evens.append(jnp.where(low, first, jnp.roll(second, CAP, axis=1)))
        odds.append(jnp.where(low, jnp.roll(first, CAP, axis=1), second))
    packed = jnp.stack([jnp.stack(evens, axis=1), jnp.stack(odds, axis=1)], axis=1)
    send[...] = packed.reshape(OWN * MSG, WIDE).astype(jnp.bfloat16)

    def block_of(ref, index):
        return ref.at[pl.ds(pl.multiple_of(index * MSG, MSG), MSG)]

    def push_blocks(*groups):
        for pair in zip(*(peers(dz) for dz in groups)):
            for dz, to in zip(groups, pair):
                push(block_of(send, to), block_of(recv, me), pay_s, pay_r.at[dz], to)

    pl.semaphore_wait(barrier, len(near) + 1)
    for to in (line[2], line[6]):
        pl.semaphore_signal(ready.at[0], inc=1, device_id=(rep, to), device_id_type=MESH)

    blocks = [
        push(
            send.at[pl.ds(pl.multiple_of(z_at[dz] * GROUP, GROUP), GROUP)], relay.at[pl.ds(i * GROUP, GROUP)],
            relay_s.at[i], relay_r.at[i], line[dz],
        )
        for i, dz in enumerate(RELAYS)
    ]

    pl.semaphore_wait(ready.at[0], 2)
    for to in x_line:
        pl.semaphore_signal(ready.at[1], inc=1, device_id=(rep, to), device_id_type=MESH)
    for dz in Z_ORDER[:-1]:
        push(code_s.at[z_at[dz] // 2], code_r.at[my_y, my_x, my_z], code_ss.at[0], code_rs.at[0], line[dz])

    def hand_on(i):
        blocks[i].wait()
        source = line[(NZ - RELAYS[i]) % NZ]
        for p, to in zip(in_plane, peers(0)):
            push(block_of(relay, i * PLANE + p), block_of(recv, source), pay_s, pay_r.at[RELAYS[i]], to)
        kept = pl.ds(pl.multiple_of(i * GROUP + in_plane[-1] * MSG, MSG), MSG)
        recv[pl.ds(pl.multiple_of(source * MSG, MSG), MSG), :] = relay[kept, :]

    pl.semaphore_wait(ready.at[1], NX - 1)
    for to in y_line:
        pl.semaphore_signal(ready.at[2], inc=1, device_id=(rep, to), device_id_type=MESH)
    pl.semaphore_wait(ready.at[2], NY - 1)
    push_blocks(0)
    push_blocks(3, 5)
    code_r[my_y, my_x, my_z] = code_s[my_z // 2]
    landed(code_r.at[0, 0], NZ - 1, code_rs.at[0])
    for dx in range(1, NX):
        part = code_r.at[my_y, my_x]
        push(part, part, code_ss.at[1], code_rs.at[1], me + (x_at[dx] - my_x) * NY)
    hand_on(0)
    hand_on(1)
    push_blocks(4)
    landed(code_r.at[0], NX - 1, code_rs.at[1])
    for dy in range(1, NY):
        part = code_r.at[my_y]
        push(part, part, code_ss.at[2], code_rs.at[2], me + y_at[dy] - my_y)
    push_blocks(1, 7)

    mine = pl.ds(pl.multiple_of(me * MSG, MSG), MSG)
    recv[mine, :] = send[mine, :]
    landed(code_r, NY - 1, code_rs.at[2])
    code_forward = push(code_r, code_r2, cfwd_s, cfwd_r, me, other)
    table = code_r[...].reshape(OWN, 128).astype(jnp.float32)
    own_code[...] = slot_column(table, base)
    query_row = slot_row_of(table, base)
    query_low = jnp.floor(query_row * (1.0 / 65536)) * 65536
    code_forward.wait()
    code_tmp[...] = slot_column(code_r2[...].reshape(OWN, 128).astype(jnp.float32), base)
    landed(code_r.at[0, 0], NZ - 1, code_ss.at[0])
    landed(code_r.at[0], NX - 1, code_ss.at[1])
    landed(code_r, NY - 1, code_ss.at[2])

    forwards = []
    for i, dz in enumerate(LAND_ORDER):
        z = z_at[(NZ - dz) % NZ]
        start = pl.multiple_of(z * GROUP, GROUP)
        slots = pl.ds(pl.multiple_of(z * TILE, TILE), TILE)
        far_code[pl.ds(i * TILE, TILE), :] = code_tmp[slots, :]
        landed(recv, GROUP - (MSG if dz in (0, *RELAYS) else 0), pay_r.at[dz])
        block = pl.ds(start, GROUP)
        forwards.append((push(recv.at[block], recv2.at[block], fwd_s.at[dz], fwd_r.at[dz], me, other), start))
        unpack_group(recv, unit_q, start, pl.multiple_of(z * TILE, TILE))

    def best_of(best, keys, code, first, count):
        similar = lax.dot_general(
            keys[pl.ds(first, count), :], unit_q[...], (((1,), (1,)), ((), ())), preferred_element_type=jnp.float32
        )
        at = code[pl.ds(first, count), 0:1]
        allowed = (at >= query_low) & (at < query_row)
        similar = jnp.where(allowed, similar, -1.0).reshape(count // 8, 8, SLOTS)
        return jnp.maximum(best, jnp.max(similar, axis=0))

    best = jnp.full((8, SLOTS), -1.0, jnp.float32)
    for first in (0, 256):
        best = best_of(best, unit_q, own_code, first, 256)
    for i, (forward, start) in enumerate(forwards):
        forward.wait()
        unpack_group(recv2, unit_k, start, i * TILE)
        if i == 3:
            best = best_of(best, unit_k, far_code, 0, 256)
        if i == 6:
            best = best_of(best, unit_k, far_code, 256, 192)
    best = best_of(best, unit_k, far_code, SLOTS - TILE, TILE)
    best = jnp.max(best, axis=0, keepdims=True)
    for c in range(4):
        res_s[c] = best[:, 128 * c : 128 * c + 128]

    for dz in Z_ORDER:
        chunk = res_s.at[z_at[dz] // 2]
        for to in peers(dz):
            push(chunk, res_r.at[me], res_ss, res_rs, to)
    res_r[me] = res_s[my_z // 2]
    landed(send, (OWN - 1 - len(RELAYS)) * MSG, pay_s)
    landed(res_r, OWN - 1, res_ss)
    landed(res_r, OWN - 1, res_rs)

    home = res_r[...].reshape(OWN, 128)
    lane = iota((OWN, 128), 1)
    owner_here = iota((OWN, ROWS), 0) == own_row
    nearest = jnp.zeros((OWN, ROWS), jnp.float32)
    for s in range(CAP):
        value = jnp.sum(jnp.where(lane == base + s, home, 0.0), axis=1, keepdims=True)
        nearest = jnp.where(owner_here & (slot_row == s), value, nearest)
    out_ref[...] = jnp.sum(nearest, axis=0, keepdims=True)


def body(embeddings, cluster, order):
    hbm = pl.BlockSpec(memory_space=pl.ANY)
    dma = pltpu.SemaphoreType.DMA
    blocks = pltpu.VMEM((OWN * MSG, WIDE), jnp.bfloat16)
    units = pltpu.VMEM((SLOTS, D), jnp.bfloat16)
    line = pltpu.VMEM((1, ROWS), jnp.int32)
    table = pltpu.VMEM((NY, NX, NZ, 1, 128), jnp.int32)
    codes = pltpu.VMEM((SLOTS, 128), jnp.float32)
    result = pl.pallas_call(
        kernel,
        out_shape=jax.ShapeDtypeStruct((1, ROWS), jnp.float32),
        in_specs=[hbm, hbm, hbm],
        out_specs=pl.BlockSpec(memory_space=pltpu.VMEM),
        scratch_shapes=[
            pltpu.VMEM((ROWS, D), jnp.bfloat16), line, line, blocks, blocks, blocks,
            pltpu.VMEM((len(RELAYS) * GROUP, WIDE), jnp.bfloat16), units, units,
            pltpu.VMEM((4, 1, 128), jnp.int32), table, table,
            pltpu.VMEM((4, 1, 128), jnp.float32), pltpu.VMEM((OWN, 1, 128), jnp.float32), codes, codes, codes,
            dma((3,)), dma, dma((NZ,)), dma((3,)), dma((3,)), dma, dma, dma((NZ,)), dma((NZ,)), dma, dma,
            dma((len(RELAYS),)), dma((len(RELAYS),)),
            pltpu.SemaphoreType.REGULAR((3,)),
        ],
        compiler_params=pltpu.CompilerParams(
            collective_id=0, has_side_effects=True, vmem_limit_bytes=VMEM_BYTES
        ),
    )(embeddings, cluster.reshape(1, ROWS), order.reshape(1, ROWS))
    return result.reshape(ROWS)


def solution(mesh):
    placed = (P(("rep", "own"), None), P(("rep", "own")), P(("rep", "own")))
    return jax.shard_map(body, mesh=mesh, in_specs=placed, out_specs=P(("rep", "own")), check_vma=False)
```

```python
import jax
import jax.numpy as jnp
from jax import lax
from jax.experimental import pallas as pl
from jax.experimental.pallas import tpu as pltpu
from jax.sharding import PartitionSpec as P

MESH = pl.DeviceIdType.MESH
CL_DEV = 4
CAP = 4
NZ, NX, NY = 8, 4, 4
OWN = NZ * NX * NY
PLANE = NX * NY
ROWS = 256
D = 1024
SLOTS = OWN * CAP
WIDE = D // 4
MSG = 16
GROUP = PLANE * MSG
TILE = PLANE * CAP
Z_ORDER = (4, 3, 5, 2, 6, 1, 7, 0)
LAND_ORDER = (0, 2, 6, 3, 5, 4, 1, 7)
RELAYS = (2, 6)
VMEM_BYTES = 55226 * 2**10
PLANE_ORDER = ((2, 2), (2, 1), (1, 2), (2, 3), (3, 2), (1, 1), (3, 3), (1, 3), (3, 1), (2, 0), (0, 2), (1, 0), (0, 1), (3, 0), (0, 3), (0, 0))


def iota(shape, dim):
    return lax.broadcasted_iota(jnp.int32, shape, dim)


def column_of(row, eye):
    return jnp.sum(jnp.where(eye, row, 0), axis=1, keepdims=True)


def exact_dot(a, b):
    return jnp.dot(a, b, precision=lax.Precision.HIGHEST, preferred_element_type=jnp.float32)


def unpack_group(src, dst, src_row, dst_row):
    block = src[pl.ds(src_row, GROUP), :].astype(jnp.float32).reshape(PLANE // 2, 2, 2, 8, WIDE)
    low = iota((1, 8, WIDE), 1) < CAP
    for half in range(2):
        even, odd = block[:, 0, half], block[:, 1, half]
        first = jnp.where(low, even, jnp.roll(odd, CAP, axis=1))
        second = jnp.where(low, jnp.roll(even, CAP, axis=1), odd)
        for i, part in enumerate((first, second)):
            lane = (2 * half + i) * WIDE
            dst[pl.ds(dst_row, TILE), lane : lane + WIDE] = part.reshape(TILE, WIDE).astype(jnp.bfloat16)


def choose(index, values):
    return sum(jnp.where(index == i, value, 0) for i, value in enumerate(values))


def source_row(slot):
    source = slot // CAP
    return (source % NY * NX + source // NY % NX) * NZ + source // PLANE


def slot_column(table, base):
    spread = (source_row(iota((SLOTS, OWN), 0)) == iota((SLOTS, OWN), 1)).astype(jnp.float32)
    pick = iota((SLOTS, 128), 1) == base + iota((SLOTS, 128), 0) % CAP
    column = jnp.sum(jnp.where(pick, exact_dot(spread, table), 0.0), axis=1, keepdims=True)
    return jnp.broadcast_to(column, (SLOTS, 128))


def slot_row_of(table, base):
    spread = (source_row(iota((OWN, SLOTS), 1)) == iota((OWN, SLOTS), 0)).astype(jnp.float32)
    pick = iota((128, SLOTS), 0) == base + iota((128, SLOTS), 1) % CAP
    return jnp.sum(jnp.where(pick, exact_dot(table.T, spread), 0.0), axis=0, keepdims=True)


def kernel(
    emb, cl_in, ord_in, out_ref,
    x_vm, cl_ref, ord_ref, send, recv, recv2, relay, unit_q, unit_k, code_s, code_r, code_r2, res_s, res_r, own_code, code_tmp, far_code,
    in_sem, pay_s, pay_r, code_ss, code_rs, res_ss, res_rs, fwd_s, fwd_r, cfwd_s, cfwd_r, relay_s, relay_r, ready,
):
    rep, me = lax.axis_index("rep"), lax.axis_index("own")
    my_z, my_x, my_y = me // PLANE, me // NY % NX, me % NY
    other = 1 - rep
    base = (me % 32) * CAP
    z_at = [(my_z + d) % NZ for d in range(NZ)]
    x_at = [(my_x + d) % NX for d in range(NX)]
    y_at = [(my_y + d) % NY for d in range(NY)]
    z_row = [z * PLANE for z in z_at]
    in_plane = [x_at[dx] * NY + y_at[dy] for dx, dy in PLANE_ORDER]

    def peers(dz):
        return [z_row[dz] + p for p in (in_plane[:-1] if dz == 0 else in_plane)]

    def push(src, dst, send_sem, recv_sem, to, core=rep):
        copy = pltpu.make_async_remote_copy(
            src_ref=src, dst_ref=dst, send_sem=send_sem, recv_sem=recv_sem, device_id=(core, to), device_id_type=MESH
        )
        copy.start()
        return copy

    def landed(ref, n, sem):
        part = ref.at[pl.ds(0, n)]
        pltpu.make_async_copy(part, part, sem).wait()

    barrier = pltpu.get_barrier_semaphore()
    column = me - my_z * PLANE
    line = [column + z_row[dz] for dz in range(NZ)]
    x_line = [me + (x_at[d] - my_x) * NY for d in range(1, NX)]
    y_line = [me + y_at[d] - my_y for d in range(1, NY)]
    near = [line[dz] for dz in (2, 6, 1, 7)] + x_line + y_line
    for to in near:
        pl.semaphore_signal(barrier, inc=1, device_id=(rep, to), device_id_type=MESH)
    pl.semaphore_signal(barrier, inc=1, device_id=(other, me), device_id_type=MESH)
    loads = [
        pltpu.make_async_copy(src, dst, in_sem.at[i])
        for i, (src, dst) in enumerate(((cl_in, cl_ref), (ord_in, ord_ref), (emb, x_vm)))
    ]
    for load in loads:
        load.start()
    for load in loads[:2]:
        load.wait()

    cl_row, ord_row = cl_ref[...], ord_ref[...]
    square = (ROWS, ROWS)
    eye = iota(square, 0) == iota(square, 1)
    own_row = cl_row // CL_DEV
    own_col = column_of(own_row, eye)
    earlier = (own_col == own_row) & (iota(square, 0) < iota(square, 1))
    slot_row = jnp.sum(earlier.astype(jnp.int32), axis=0, keepdims=True)
    placed_row = own_row * CAP + slot_row
    loads[2].wait()
    values = x_vm[...].astype(jnp.float32)
    scale = lax.rsqrt(jnp.sum(values * values, axis=1, keepdims=True) + 1e-06)
    unit = (values * scale).astype(jnp.bfloat16)
    low = iota((1, 8, WIDE), 1) < CAP

    def pack(*groups):
        count = len(groups) * TILE
        index = iota((count, ROWS), 0)
        slot = choose(index // TILE, [z_at[dz] * TILE for dz in groups]) + index % TILE
        place = (slot == placed_row).astype(jnp.bfloat16)
        evens, odds = [], []
        for half in range(2):
            first, second = (
                jnp.dot(place, unit[:, q * WIDE : (q + 1) * WIDE], preferred_element_type=jnp.float32).reshape(
                    count // 8, 8, WIDE
                )
                for q in (2 * half, 2 * half + 1)
            )
            evens.append(jnp.where(low, first, jnp.roll(second, CAP, axis=1)))
            odds.append(jnp.where(low, jnp.roll(first, CAP, axis=1), second))
        packed = jnp.stack([jnp.stack(evens, axis=1), jnp.stack(odds, axis=1)], axis=1)
        packed = packed.reshape(len(groups), GROUP, WIDE).astype(jnp.bfloat16)
        for i, dz in enumerate(groups):
            send[pl.ds(pl.multiple_of(z_at[dz] * GROUP, GROUP), GROUP), :] = packed[i]

    pack(*RELAYS)

    def block_of(ref, index):
        return ref.at[pl.ds(pl.multiple_of(index * MSG, MSG), MSG)]

    def push_blocks(*groups):
        for pair in zip(*(peers(dz) for dz in groups)):
            for dz, to in zip(groups, pair):
                push(block_of(send, to), block_of(recv, me), pay_s, pay_r.at[dz], to)

    pl.semaphore_wait(barrier, len(near) + 1)
    for to in (line[2], line[6]):
        pl.semaphore_signal(ready.at[0], inc=1, device_id=(rep, to), device_id_type=MESH)

    blocks = [
        push(
            send.at[pl.ds(pl.multiple_of(z_at[dz] * GROUP, GROUP), GROUP)], relay.at[pl.ds(i * GROUP, GROUP)],
            relay_s.at[i], relay_r.at[i], line[dz],
        )
        for i, dz in enumerate(RELAYS)
    ]

    code_row = (cl_row % CL_DEV) * 65536 + ord_row
    placed_col = column_of(placed_row, eye)
    code_col = column_of(code_row, eye)
    sent = placed_col == iota((ROWS, SLOTS), 1)
    codes = jnp.sum(jnp.where(sent, code_col + 1, 0), axis=0, keepdims=True) - 1
    for c in range(4):
        code_s[c] = codes[:, 128 * c : 128 * c + 128]
    pl.semaphore_wait(ready.at[0], 2)
    for to in x_line:
        pl.semaphore_signal(ready.at[1], inc=1, device_id=(rep, to), device_id_type=MESH)
    for dz in Z_ORDER[:-1]:
        push(code_s.at[z_at[dz] // 2], code_r.at[my_y, my_x, my_z], code_ss.at[0], code_rs.at[0], line[dz])

    pack(*(dz for dz in range(NZ) if dz not in RELAYS))

    def hand_on(i):
        blocks[i].wait()
        source = line[(NZ - RELAYS[i]) % NZ]
        for p, to in zip(in_plane, peers(0)):
            push(block_of(relay, i * PLANE + p), block_of(recv, source), pay_s, pay_r.at[RELAYS[i]], to)
        kept = pl.ds(pl.multiple_of(i * GROUP + in_plane[-1] * MSG, MSG), MSG)
        recv[pl.ds(pl.multiple_of(source * MSG, MSG), MSG), :] = relay[kept, :]

    pl.semaphore_wait(ready.at[1], NX - 1)
    for to in y_line:
        pl.semaphore_signal(ready.at[2], inc=1, device_id=(rep, to), device_id_type=MESH)
    pl.semaphore_wait(ready.at[2], NY - 1)
    push_blocks(0)
    push_blocks(3, 5)
    code_r[my_y, my_x, my_z] = code_s[my_z // 2]
    landed(code_r.at[0, 0], NZ - 1, code_rs.at[0])
    for dx in range(1, NX):
        part = code_r.at[my_y, my_x]
        push(part, part, code_ss.at[1], code_rs.at[1], me + (x_at[dx] - my_x) * NY)
    hand_on(0)
    hand_on(1)
    push_blocks(4)
    landed(code_r.at[0], NX - 1, code_rs.at[1])
    for dy in range(1, NY):
        part = code_r.at[my_y]
        push(part, part, code_ss.at[2], code_rs.at[2], me + y_at[dy] - my_y)
    push_blocks(1, 7)

    mine = pl.ds(pl.multiple_of(me * MSG, MSG), MSG)
    recv[mine, :] = send[mine, :]
    landed(code_r, NY - 1, code_rs.at[2])
    code_forward = push(code_r, code_r2, cfwd_s, cfwd_r, me, other)
    table = code_r[...].reshape(OWN, 128).astype(jnp.float32)
    own_code[...] = slot_column(table, base)
    query_row = slot_row_of(table, base)
    query_low = jnp.floor(query_row * (1.0 / 65536)) * 65536
    code_forward.wait()
    code_tmp[...] = slot_column(code_r2[...].reshape(OWN, 128).astype(jnp.float32), base)
    landed(code_r.at[0, 0], NZ - 1, code_ss.at[0])
    landed(code_r.at[0], NX - 1, code_ss.at[1])
    landed(code_r, NY - 1, code_ss.at[2])

    forwards = []
    for i, dz in enumerate(LAND_ORDER):
        z = z_at[(NZ - dz) % NZ]
        start = pl.multiple_of(z * GROUP, GROUP)
        slots = pl.ds(pl.multiple_of(z * TILE, TILE), TILE)
        far_code[pl.ds(i * TILE, TILE), :] = code_tmp[slots, :]
        landed(recv, GROUP - (MSG if dz in (0, *RELAYS) else 0), pay_r.at[dz])
        block = pl.ds(start, GROUP)
        forwards.append((push(recv.at[block], recv2.at[block], fwd_s.at[dz], fwd_r.at[dz], me, other), start))
        unpack_group(recv, unit_q, start, pl.multiple_of(z * TILE, TILE))

    def best_of(best, keys, code, first, count):
        similar = lax.dot_general(
            keys[pl.ds(first, count), :], unit_q[...], (((1,), (1,)), ((), ())), preferred_element_type=jnp.float32
        )
        at = code[pl.ds(first, count), 0:1]
        allowed = (at >= query_low) & (at < query_row)
        similar = jnp.where(allowed, similar, -1.0).reshape(count // 8, 8, SLOTS)
        return jnp.maximum(best, jnp.max(similar, axis=0))

    best = jnp.full((8, SLOTS), -1.0, jnp.float32)
    for first in (0, 256):
        best = best_of(best, unit_q, own_code, first, 256)
    for i, (forward, start) in enumerate(forwards):
        forward.wait()
        unpack_group(recv2, unit_k, start, i * TILE)
        if i == 3:
            best = best_of(best, unit_k, far_code, 0, 256)
        if i == 6:
            best = best_of(best, unit_k, far_code, 256, 192)
    best = best_of(best, unit_k, far_code, SLOTS - TILE, TILE)
    best = jnp.max(best, axis=0, keepdims=True)
    for c in range(4):
        res_s[c] = best[:, 128 * c : 128 * c + 128]

    for dz in Z_ORDER:
        chunk = res_s.at[z_at[dz] // 2]
        for to in peers(dz):
            push(chunk, res_r.at[me], res_ss, res_rs, to)
    res_r[me] = res_s[my_z // 2]
    landed(send, (OWN - 1 - len(RELAYS)) * MSG, pay_s)
    landed(res_r, OWN - 1, res_ss)
    landed(res_r, OWN - 1, res_rs)

    home = res_r[...].reshape(OWN, 128)
    lane = iota((OWN, 128), 1)
    owner_here = iota((OWN, ROWS), 0) == own_row
    nearest = jnp.zeros((OWN, ROWS), jnp.float32)
    for s in range(CAP):
        value = jnp.sum(jnp.where(lane == base + s, home, 0.0), axis=1, keepdims=True)
        nearest = jnp.where(owner_here & (slot_row == s), value, nearest)
    out_ref[...] = jnp.sum(nearest, axis=0, keepdims=True)


def body(embeddings, cluster, order):
    hbm = pl.BlockSpec(memory_space=pl.ANY)
    dma = pltpu.SemaphoreType.DMA
    blocks = pltpu.VMEM((OWN * MSG, WIDE), jnp.bfloat16)
    units = pltpu.VMEM((SLOTS, D), jnp.bfloat16)
    line = pltpu.VMEM((1, ROWS), jnp.int32)
    table = pltpu.VMEM((NY, NX, NZ, 1, 128), jnp.int32)
    codes = pltpu.VMEM((SLOTS, 128), jnp.float32)
    result = pl.pallas_call(
        kernel,
        out_shape=jax.ShapeDtypeStruct((1, ROWS), jnp.float32),
        in_specs=[hbm, hbm, hbm],
        out_specs=pl.BlockSpec(memory_space=pltpu.VMEM),
        scratch_shapes=[
            pltpu.VMEM((ROWS, D), jnp.bfloat16), line, line, blocks, blocks, blocks,
            pltpu.VMEM((len(RELAYS) * GROUP, WIDE), jnp.bfloat16), units, units,
            pltpu.VMEM((4, 1, 128), jnp.int32), table, table,
            pltpu.VMEM((4, 1, 128), jnp.float32), pltpu.VMEM((OWN, 1, 128), jnp.float32), codes, codes, codes,
            dma((3,)), dma, dma((NZ,)), dma((3,)), dma((3,)), dma, dma, dma((NZ,)), dma((NZ,)), dma, dma,
            dma((len(RELAYS),)), dma((len(RELAYS),)),
            pltpu.SemaphoreType.REGULAR((3,)),
        ],
        compiler_params=pltpu.CompilerParams(
            collective_id=0, has_side_effects=True, vmem_limit_bytes=VMEM_BYTES
        ),
    )(embeddings, cluster.reshape(1, ROWS), order.reshape(1, ROWS))
    return result.reshape(ROWS)


def solution(mesh):
    placed = (P(("rep", "own"), None), P(("rep", "own")), P(("rep", "own")))
    return jax.shard_map(body, mesh=mesh, in_specs=placed, out_specs=P(("rep", "own")), check_vma=False)
```

```python
import jax
import jax.numpy as jnp
from jax import lax
from jax.experimental import pallas as pl
from jax.experimental.pallas import tpu as pltpu
from jax.sharding import PartitionSpec as P

MESH = pl.DeviceIdType.MESH
CL_DEV = 4
CAP = 4
NZ, NX, NY = 8, 4, 4
OWN = NZ * NX * NY
PLANE = NX * NY
ROWS = 256
D = 1024
SLOTS = OWN * CAP
WIDE = D // 4
MSG = 16
GROUP = PLANE * MSG
TILE = PLANE * CAP
Z_ORDER = (4, 3, 5, 2, 6, 1, 7, 0)
LAND_ORDER = (0, 2, 6, 3, 5, 4, 1, 7)
RELAYS = (2, 6)
VMEM_BYTES = 55226 * 2**10
PLANE_ORDER = ((2, 2), (2, 1), (1, 2), (2, 3), (3, 2), (1, 1), (3, 3), (1, 3), (3, 1), (2, 0), (0, 2), (1, 0), (0, 1), (3, 0), (0, 3), (0, 0))


def iota(shape, dim):
    return lax.broadcasted_iota(jnp.int32, shape, dim)


def column_of(row, eye):
    return jnp.sum(jnp.where(eye, row, 0), axis=1, keepdims=True)


def exact_dot(a, b):
    return jnp.dot(a, b, precision=lax.Precision.HIGHEST, preferred_element_type=jnp.float32)


def unpack_group(src, dst, src_row, dst_row):
    block = src[pl.ds(src_row, GROUP), :].astype(jnp.float32).reshape(PLANE // 2, 2, 2, 8, WIDE)
    low = iota((1, 8, WIDE), 1) < CAP
    for half in range(2):
        even, odd = block[:, 0, half], block[:, 1, half]
        first = jnp.where(low, even, jnp.roll(odd, CAP, axis=1))
        second = jnp.where(low, jnp.roll(even, CAP, axis=1), odd)
        for i, part in enumerate((first, second)):
            lane = (2 * half + i) * WIDE
            dst[pl.ds(dst_row, TILE), lane : lane + WIDE] = part.reshape(TILE, WIDE).astype(jnp.bfloat16)


def source_row(slot):
    source = slot // CAP
    return (source % NY * NX + source // NY % NX) * NZ + source // PLANE


def slot_column(table, base):
    spread = (source_row(iota((SLOTS, OWN), 0)) == iota((SLOTS, OWN), 1)).astype(jnp.float32)
    pick = iota((SLOTS, 128), 1) == base + iota((SLOTS, 128), 0) % CAP
    column = jnp.sum(jnp.where(pick, exact_dot(spread, table), 0.0), axis=1, keepdims=True)
    return jnp.broadcast_to(column, (SLOTS, 128))


def slot_row_of(table, base):
    spread = (source_row(iota((OWN, SLOTS), 1)) == iota((OWN, SLOTS), 0)).astype(jnp.float32)
    pick = iota((128, SLOTS), 0) == base + iota((128, SLOTS), 1) % CAP
    return jnp.sum(jnp.where(pick, exact_dot(table.T, spread), 0.0), axis=0, keepdims=True)


def kernel(
    emb, cl_in, ord_in, out_ref,
    x_vm, cl_ref, ord_ref, send, recv, recv2, relay, unit_q, unit_k, code_s, code_r, code_r2, res_s, res_r, own_code, code_tmp, far_code,
    in_sem, pay_s, pay_r, code_ss, code_rs, res_ss, res_rs, fwd_s, fwd_r, cfwd_s, cfwd_r, relay_s, relay_r, ready,
):
    rep, me = lax.axis_index("rep"), lax.axis_index("own")
    my_z, my_x, my_y = me // PLANE, me // NY % NX, me % NY
    other = 1 - rep
    base = (me % 32) * CAP
    z_at = [(my_z + d) % NZ for d in range(NZ)]
    x_at = [(my_x + d) % NX for d in range(NX)]
    y_at = [(my_y + d) % NY for d in range(NY)]
    z_row = [z * PLANE for z in z_at]
    in_plane = [x_at[dx] * NY + y_at[dy] for dx, dy in PLANE_ORDER]

    def peers(dz):
        return [z_row[dz] + p for p in (in_plane[:-1] if dz == 0 else in_plane)]

    def push(src, dst, send_sem, recv_sem, to, core=rep):
        copy = pltpu.make_async_remote_copy(
            src_ref=src, dst_ref=dst, send_sem=send_sem, recv_sem=recv_sem, device_id=(core, to), device_id_type=MESH
        )
        copy.start()
        return copy

    def landed(ref, n, sem):
        part = ref.at[pl.ds(0, n)]
        pltpu.make_async_copy(part, part, sem).wait()

    barrier = pltpu.get_barrier_semaphore()
    column = me - my_z * PLANE
    line = [column + z_row[dz] for dz in range(NZ)]
    x_line = [me + (x_at[d] - my_x) * NY for d in range(1, NX)]
    y_line = [me + y_at[d] - my_y for d in range(1, NY)]
    near = [line[dz] for dz in (2, 6, 1, 7)] + x_line + y_line
    for to in near:
        pl.semaphore_signal(barrier, inc=1, device_id=(rep, to), device_id_type=MESH)
    pl.semaphore_signal(barrier, inc=1, device_id=(other, me), device_id_type=MESH)
    loads = [
        pltpu.make_async_copy(src, dst, in_sem.at[i])
        for i, (src, dst) in enumerate(((cl_in, cl_ref), (ord_in, ord_ref), (emb, x_vm)))
    ]
    for load in loads:
        load.start()
    for load in loads[:2]:
        load.wait()

    cl_row, ord_row = cl_ref[...], ord_ref[...]
    square = (ROWS, ROWS)
    eye = iota(square, 0) == iota(square, 1)
    own_row = cl_row // CL_DEV
    own_col = column_of(own_row, eye)
    earlier = (own_col == own_row) & (iota(square, 0) < iota(square, 1))
    slot_row = jnp.sum(earlier.astype(jnp.int32), axis=0, keepdims=True)
    placed_row = own_row * CAP + slot_row
    code_row = (cl_row % CL_DEV) * 65536 + ord_row
    placed_col = column_of(placed_row, eye)
    code_col = column_of(code_row, eye)
    sent = placed_col == iota((ROWS, SLOTS), 1)
    codes = jnp.sum(jnp.where(sent, code_col + 1, 0), axis=0, keepdims=True) - 1
    for c in range(4):
        code_s[c] = codes[:, 128 * c : 128 * c + 128]

    loads[2].wait()
    values = x_vm[...].astype(jnp.float32)
    scale = lax.rsqrt(jnp.sum(values * values, axis=1, keepdims=True) + 1e-06)
    unit = (values * scale).astype(jnp.bfloat16)
    place = (iota((SLOTS, ROWS), 0) == placed_row).astype(jnp.bfloat16)
    low = iota((1, 8, WIDE), 1) < CAP
    evens, odds = [], []
    for half in range(2):
        first, second = (
            jnp.dot(place, unit[:, q * WIDE : (q + 1) * WIDE], preferred_element_type=jnp.float32).reshape(
                OWN // 2, 8, WIDE
            )
            for q in (2 * half, 2 * half + 1)
        )
        evens.append(jnp.where(low, first, jnp.roll(second, CAP, axis=1)))
        odds.append(jnp.where(low, jnp.roll(first, CAP, axis=1), second))
    packed = jnp.stack([jnp.stack(evens, axis=1), jnp.stack(odds, axis=1)], axis=1)
    send[...] = packed.reshape(OWN * MSG, WIDE).astype(jnp.bfloat16)

    def block_of(ref, index):
        return ref.at[pl.ds(pl.multiple_of(index * MSG, MSG), MSG)]

    def push_blocks(*groups):
        for pair in zip(*(peers(dz) for dz in groups)):
            for dz, to in zip(groups, pair):
                push(block_of(send, to), block_of(recv, me), pay_s, pay_r.at[dz], to)

    pl.semaphore_wait(barrier, len(near) + 1)
    for to in (line[2], line[6]):
        pl.semaphore_signal(ready.at[0], inc=1, device_id=(rep, to), device_id_type=MESH)

    blocks = [
        push(
            send.at[pl.ds(pl.multiple_of(z_at[dz] * GROUP, GROUP), GROUP)], relay.at[pl.ds(i * GROUP, GROUP)],
            relay_s.at[i], relay_r.at[i], line[dz],
        )
        for i, dz in enumerate(RELAYS)
    ]

    pl.semaphore_wait(ready.at[0], 2)
    for to in x_line:
        pl.semaphore_signal(ready.at[1], inc=1, device_id=(rep, to), device_id_type=MESH)
    for dz in Z_ORDER[:-1]:
        push(code_s.at[z_at[dz] // 2], code_r.at[my_y, my_x, my_z], code_ss.at[0], code_rs.at[0], line[dz])

    def hand_on(i):
        blocks[i].wait()
        source = line[(NZ - RELAYS[i]) % NZ]
        for p, to in zip(in_plane, peers(0)):
            push(block_of(relay, i * PLANE + p), block_of(recv, source), pay_s, pay_r.at[RELAYS[i]], to)
        kept = pl.ds(pl.multiple_of(i * GROUP + in_plane[-1] * MSG, MSG), MSG)
        recv[pl.ds(pl.multiple_of(source * MSG, MSG), MSG), :] = relay[kept, :]

    pl.semaphore_wait(ready.at[1], NX - 1)
    for to in y_line:
        pl.semaphore_signal(ready.at[2], inc=1, device_id=(rep, to), device_id_type=MESH)
    pl.semaphore_wait(ready.at[2], NY - 1)
    push_blocks(0)
    push_blocks(3, 5)
    code_r[my_y, my_x, my_z] = code_s[my_z // 2]
    landed(code_r.at[0, 0], NZ - 1, code_rs.at[0])
    for dx in range(1, NX):
        part = code_r.at[my_y, my_x]
        push(part, part, code_ss.at[1], code_rs.at[1], me + (x_at[dx] - my_x) * NY)
    hand_on(0)
    hand_on(1)
    push_blocks(4)
    landed(code_r.at[0], NX - 1, code_rs.at[1])
    for dy in range(1, NY):
        part = code_r.at[my_y]
        push(part, part, code_ss.at[2], code_rs.at[2], me + y_at[dy] - my_y)
    push_blocks(1, 7)

    mine = pl.ds(pl.multiple_of(me * MSG, MSG), MSG)
    recv[mine, :] = send[mine, :]
    landed(code_r, NY - 1, code_rs.at[2])
    code_forward = push(code_r, code_r2, cfwd_s, cfwd_r, me, other)
    table = code_r[...].reshape(OWN, 128).astype(jnp.float32)
    own_code[...] = slot_column(table, base)
    query_row = slot_row_of(table, base)
    query_low = jnp.floor(query_row * (1.0 / 65536)) * 65536
    code_forward.wait()
    code_tmp[...] = slot_column(code_r2[...].reshape(OWN, 128).astype(jnp.float32), base)
    landed(code_r.at[0, 0], NZ - 1, code_ss.at[0])
    landed(code_r.at[0], NX - 1, code_ss.at[1])
    landed(code_r, NY - 1, code_ss.at[2])

    forwards = []
    for i, dz in enumerate(LAND_ORDER):
        z = z_at[(NZ - dz) % NZ]
        start = pl.multiple_of(z * GROUP, GROUP)
        slots = pl.ds(pl.multiple_of(z * TILE, TILE), TILE)
        far_code[pl.ds(i * TILE, TILE), :] = code_tmp[slots, :]
        landed(recv, GROUP - (MSG if dz in (0, *RELAYS) else 0), pay_r.at[dz])
        block = pl.ds(start, GROUP)
        forwards.append((push(recv.at[block], recv2.at[block], fwd_s.at[dz], fwd_r.at[dz], me, other), start))
        unpack_group(recv, unit_q, start, pl.multiple_of(z * TILE, TILE))

    def best_of(best, keys, code, first, count):
        similar = lax.dot_general(
            keys[pl.ds(first, count), :], unit_q[...], (((1,), (1,)), ((), ())), preferred_element_type=jnp.float32
        )
        at = code[pl.ds(first, count), 0:1]
        allowed = (at >= query_low) & (at < query_row)
        similar = jnp.where(allowed, similar, -1.0).reshape(count // 8, 8, SLOTS)
        return jnp.maximum(best, jnp.max(similar, axis=0))

    best = jnp.full((8, SLOTS), -1.0, jnp.float32)
    for first in (0, 256):
        best = best_of(best, unit_q, own_code, first, 256)
    for i, (forward, start) in enumerate(forwards):
        forward.wait()
        unpack_group(recv2, unit_k, start, i * TILE)
        if i == 3:
            best = best_of(best, unit_k, far_code, 0, 256)
        if i == 6:
            best = best_of(best, unit_k, far_code, 256, 192)
    best = best_of(best, unit_k, far_code, SLOTS - TILE, TILE)
    best = jnp.max(best, axis=0, keepdims=True)
    for c in range(4):
        res_s[c] = best[:, 128 * c : 128 * c + 128]

    for dz in Z_ORDER:
        chunk = res_s.at[z_at[dz] // 2]
        for to in peers(dz):
            push(chunk, res_r.at[me], res_ss, res_rs, to)
    res_r[me] = res_s[my_z // 2]
    landed(res_r, OWN - 1, res_rs)

    home = res_r[...].reshape(OWN, 128)
    lane = iota((OWN, 128), 1)
    owner_here = iota((OWN, ROWS), 0) == own_row
    nearest = jnp.zeros((OWN, ROWS), jnp.float32)
    for s in range(CAP):
        value = jnp.sum(jnp.where(lane == base + s, home, 0.0), axis=1, keepdims=True)
        nearest = jnp.where(owner_here & (slot_row == s), value, nearest)
    out_ref[...] = jnp.sum(nearest, axis=0, keepdims=True)
    landed(send, (OWN - 1 - len(RELAYS)) * MSG, pay_s)
    landed(res_r, OWN - 1, res_ss)


def body(embeddings, cluster, order):
    hbm = pl.BlockSpec(memory_space=pl.ANY)
    dma = pltpu.SemaphoreType.DMA
    blocks = pltpu.VMEM((OWN * MSG, WIDE), jnp.bfloat16)
    units = pltpu.VMEM((SLOTS, D), jnp.bfloat16)
    line = pltpu.VMEM((1, ROWS), jnp.int32)
    table = pltpu.VMEM((NY, NX, NZ, 1, 128), jnp.int32)
    codes = pltpu.VMEM((SLOTS, 128), jnp.float32)
    result = pl.pallas_call(
        kernel,
        out_shape=jax.ShapeDtypeStruct((1, ROWS), jnp.float32),
        in_specs=[hbm, hbm, hbm],
        out_specs=pl.BlockSpec(memory_space=pltpu.VMEM),
        scratch_shapes=[
            pltpu.VMEM((ROWS, D), jnp.bfloat16), line, line, blocks, blocks, blocks,
            pltpu.VMEM((len(RELAYS) * GROUP, WIDE), jnp.bfloat16), units, units,
            pltpu.VMEM((4, 1, 128), jnp.int32), table, table,
            pltpu.VMEM((4, 1, 128), jnp.float32), pltpu.VMEM((OWN, 1, 128), jnp.float32), codes, codes, codes,
            dma((3,)), dma, dma((NZ,)), dma((3,)), dma((3,)), dma, dma, dma((NZ,)), dma((NZ,)), dma, dma,
            dma((len(RELAYS),)), dma((len(RELAYS),)),
            pltpu.SemaphoreType.REGULAR((3,)),
        ],
        compiler_params=pltpu.CompilerParams(
            collective_id=0, has_side_effects=True, vmem_limit_bytes=VMEM_BYTES
        ),
    )(embeddings, cluster.reshape(1, ROWS), order.reshape(1, ROWS))
    return result.reshape(ROWS)


def solution(mesh):
    placed = (P(("rep", "own"), None), P(("rep", "own")), P(("rep", "own")))
    return jax.shard_map(body, mesh=mesh, in_specs=placed, out_specs=P(("rep", "own")), check_vma=False)
```
